32 devices in a mesh: gx: 8 (over z, core), gy: 4 (over y, x).
Axes of the slice: x: 2, y: 2, z: 4, core: 2. Of those that a mesh axis runs over, the one named last changes fastest.
Arguments:
- coil_sources: float32 [8, 128, 128, 128], P(None, 'gx', 'gy'), may hold values from -6 to 6
- tissue_labels: int32 [128, 128, 128], P('gx', 'gy'), may hold values from 0 to 5
- class_conductivity: float32 [6], replicated, may hold values from 0.1 to 2
Outputs:
- potential: float32 [8, 128, 128, 128], P(None, 'gx', 'gy')
The draws below stay inside these ranges and needn't reach their ends.
All inputs are finite; a program needn't handle non-finite values.
Results may differ from the reference program's by a relative error of at most 0.0003.
Values sent between devices are 32-bit elements; how exact they have to be, the bound alone decides.
A program may use at most 192 MiB of HBM per device.

```python
import math
import jax
import jax.numpy as jnp
from jax import lax

R = 8
NZ = 128
LEVELS = 5
SWEEPS = 2
COARSE_SWEEPS = 16
CLASSES = 6
NX = 128
NY = 128


def draw_coil_sources(key, part):
    values = jax.random.normal(key, (R, NX, NY, NZ), jnp.float32)
    return jnp.clip(values, -6.0, 6.0)


def plant(entries, rng, least, largest):
    longest = entries.shape.index(max(entries.shape))
    spots = []
    for shift in (0, 1):
        where = [jax.random.randint(jax.random.fold_in(rng, axis), (), 0, length) for axis, length in enumerate(entries.shape)]
        where[longest] = (where[longest] + shift) % entries.shape[longest]
        spots.append(tuple(where))
    return entries.at[spots[0]].set(least).at[spots[1]].set(largest)


def setup_inputs(seed: int = 0) -> dict:
    arg_keys = jax.random.split(jax.random.key(seed), 4)
    return {
        "coil_sources": draw_coil_sources(jax.random.fold_in(arg_keys[3], 71), 0),
        "tissue_labels": plant(jax.random.randint(arg_keys[1], (NX, NY, NZ), 0, CLASSES), jax.random.fold_in(arg_keys[1], 1), 0, CLASSES - 1).astype(jnp.int32),
        "class_conductivity": jnp.clip(jnp.exp(jax.random.uniform(arg_keys[2], (CLASSES,), jnp.float32, math.log(0.1), math.log(2.0))), 0.1, 2.0),
    }


damping = 0.8


def lookup_table(labels, table):
    result = jnp.zeros(labels.shape, jnp.float32)
    for klass in range(CLASSES):
        result = result + jnp.where(labels == klass, table[klass], jnp.float32(0.0))
    return result


def coarsen_cond(cond):
    sx, sy, sz = cond.shape
    return cond.reshape(sx // 2, 2, sy // 2, 2, sz // 2, 2).mean(axis=(1, 3, 5))


def restrict_sum(field):
    rr, sx, sy, sz = field.shape
    return field.reshape(rr, sx // 2, 2, sy // 2, 2, sz // 2, 2).sum(axis=(2, 4, 6))


def prolong_copy(field):
    rr, sx, sy, sz = field.shape
    grown = jnp.broadcast_to(field[:, :, None, :, None, :, None], (rr, sx, 2, sy, 2, sz, 2))
    return grown.reshape(rr, 2 * sx, 2 * sy, 2 * sz)


def face_coeffs(extended):
    centre = extended[1:-1, 1:-1, :]
    zpadded = jnp.pad(centre, ((0, 0), (0, 0), (1, 1)))
    others = [extended[2:, 1:-1, :], extended[:-2, 1:-1, :], extended[1:-1, 2:, :],
              extended[1:-1, :-2, :], zpadded[:, :, 2:], zpadded[:, :, :-2]]
    coeffs = [jnp.where(other > 0, 2.0 * centre * other / (centre + other), centre) for other in others]
    face_sum = coeffs[0] + coeffs[1] + coeffs[2] + coeffs[3] + coeffs[4] + coeffs[5]
    return coeffs, face_sum


def apply_operator(extended, field, coeffs, face_sum, scale):
    zpadded = jnp.pad(field, ((0, 0), (0, 0), (0, 0), (1, 1)))
    others = [extended[:, 2:, 1:-1, :], extended[:, :-2, 1:-1, :], extended[:, 1:-1, 2:, :],
              extended[:, 1:-1, :-2, :], zpadded[:, :, :, 2:], zpadded[:, :, :, :-2]]
    total = coeffs[0] * others[0]
    for index in range(1, 6):
        total = total + coeffs[index] * others[index]
    return scale * (face_sum * field - total)


def pad_field(field):
    return jnp.pad(field, ((0, 0), (1, 1), (1, 1), (0, 0)))


def pad_cond(cond):
    return jnp.pad(cond, ((1, 1), (1, 1), (0, 0)))


def relax(field, source, coeffs, face_sum, scale, count):
    diagonal = scale * face_sum
    for sweep_index in range(count):
        field = field + damping * (source - apply_operator(pad_field(field), field, coeffs, face_sum, scale)) / diagonal
    return field


def vcycle(level, source, conductivities):
    scale = jnp.float32(2.0 ** level)
    coeffs, face_sum = face_coeffs(pad_cond(conductivities[level]))
    diagonal = scale * face_sum
    field = damping * source / diagonal
    if level == LEVELS - 1:
        return relax(field, source, coeffs, face_sum, scale, COARSE_SWEEPS - 1)
    field = relax(field, source, coeffs, face_sum, scale, SWEEPS - 1)
    residual = source - apply_operator(pad_field(field), field, coeffs, face_sum, scale)
    correction = vcycle(level + 1, restrict_sum(residual), conductivities)
    field = field + prolong_copy(correction)
    return relax(field, source, coeffs, face_sum, scale, SWEEPS)


def reference(coil_sources, tissue_labels, class_conductivity):
    conductivities = [lookup_table(tissue_labels, class_conductivity)]
    for level in range(LEVELS - 1):
        conductivities.append(coarsen_cond(conductivities[-1]))

    def one_source(source):
        return vcycle(0, source[None], conductivities)[0]

    return lax.map(one_source, coil_sources)
```

```python
import functools

import jax
import jax.numpy as jnp
from jax import lax
from jax.experimental import pallas as pl
from jax.experimental.pallas import tpu as pltpu
from jax.sharding import PartitionSpec as P

CLASSES = 6
SWEEPS_COARSE = 16
DAMP = 0.8
KEEP = 1.0 - DAMP
MESH = pl.DeviceIdType.MESH
DIRS = [(dx, dy) for dx in (-1, 0, 1) for dy in (-1, 0, 1) if (dx, dy) != (0, 0)]
ROWS = 8


def iota(shape, dim):
    return lax.broadcasted_iota(jnp.int32, shape, dim)


def roll(t, shift, axis):
    return pltpu.roll(t, shift % t.shape[axis], axis)


def pairsum(t, step, axis):
    even = (iota(t.shape, axis) // step) % 2 == 0
    return t + jnp.where(even, roll(t, -step, axis), roll(t, step, axis))


def harmonic(a, b):
    return 2.0 * a * b / (a + b)


class Level:
    def __init__(self, index, bx, by, nz, halo, chalo):
        self.bx, self.by, self.nz = bx, by, nz
        self.h, self.hc, self.step = halo, chalo, 2**index
        self.vshape = (bx + 2 * halo, by + 2 * halo, 8, nz)
        self.cshape = (bx + 2 * chalo, by + 2 * ROWS, nz)


def exchange(src, dst, offs, dims, widths, sems, axes, src_offs=None):
    me, count = axes
    src_offs = offs if src_offs is None else src_offs
    copies = []
    for d, step in enumerate(DIRS):
        s_idx, d_idx = [], []
        for k in (0, 1):
            so, o, n, w = src_offs[k], offs[k], dims[k], widths[k]
            if step[k] == 0:
                s_idx.append(pl.ds(so, n))
                d_idx.append(pl.ds(o, n))
            elif step[k] < 0:
                s_idx.append(pl.ds(so, w))
                d_idx.append(pl.ds(o + n, w))
            else:
                s_idx.append(pl.ds(so + n - w, w))
                d_idx.append(pl.ds(o - w, w))
        target = tuple(lax.rem(me[k] + step[k] + count[k], count[k]) for k in (0, 1))
        copies.append(
            pltpu.make_async_remote_copy(
                src_ref=src.at[tuple(s_idx)],
                dst_ref=dst.at[tuple(d_idx)],
                send_sem=sems.at[0, d],
                recv_sem=sems.at[1, d],
                device_id=target,
                device_id_type=MESH,
            )
        )
    for copy in copies:
        copy.start()
    return copies


def finish(copies):
    for copy in copies:
        copy.wait()


def coefficients(lev, c, kx, ky, kz, kk, ww, me, count):
    rows = lev.cshape[1]
    shape = (rows, lev.nz)
    ycell = iota(shape, 0) - ROWS + me[1] * lev.by
    ylast = count[1] * lev.by - 1
    zlane = iota(shape, 1)
    zfirst, zlast = zlane < lev.step, zlane >= lev.nz - lev.step
    xlast = count[0] * lev.bx - 1
    xbase = me[0] * lev.bx - lev.hc

    def faces(x, carry):
        cc = c[x]
        cell = x + xbase
        xk = jnp.where(jnp.logical_or(cell == 0, cell == xlast + 1), 0.0, harmonic(cc, c[x - 1]))
        kx[x] = xk
        ky[x] = jnp.where(
            jnp.logical_or(ycell == 0, ycell == ylast + 1), 0.0, harmonic(cc, roll(cc, 1, 0))
        )
        kz[x] = jnp.where(zlast, 0.0, harmonic(cc, roll(cc, -lev.step, 1)))
        return carry

    lax.fori_loop(1, lev.cshape[0], faces, 0)

    def sums(x, carry):
        cc = c[x]
        cell = x + xbase
        yk, zk = ky[x], kz[x]
        total = jnp.where(cell == 0, cc, kx[x]) + jnp.where(cell == xlast, cc, kx[x + 1])
        total = total + jnp.where(ycell == 0, cc, yk) + jnp.where(ycell == ylast, cc, roll(yk, -1, 0))
        total = total + jnp.where(zlast, cc, zk) + jnp.where(zfirst, cc, roll(zk, lev.step, 1))
        kk[x] = total
        ww[x] = DAMP / total
        return carry

    lax.fori_loop(1, lev.cshape[0] - 1, sums, 0)


def row_pass(lev, co, v, x, ys, emit):
    kx, ky, kz, kk, ww = co
    xc = x + lev.hc - lev.h
    held, faces = {}, {}

    def value(y):
        if y not in held:
            held[y] = v[x, y]
        return held[y]

    def at(ref, xx, y):
        yy = y + ROWS - lev.h
        return ref[xx, yy : yy + 1, :]

    def yface(y):
        if y not in faces:
            faces[y] = at(ky, xc, y)
        return faces[y]

    for y in ys:
        here = value(y)
        zk = at(kz, xc, y)
        total = at(kx, xc, y) * v[x - 1, y] + at(kx, xc + 1, y) * v[x + 1, y]
        total = total + yface(y) * value(y - 1) + yface(y + 1) * value(y + 1)
        total = total + zk * roll(here, -lev.step, 1) + roll(zk * here, lev.step, 1)
        emit(y, here, total, functools.partial(at, xx=xc, y=y))


def spans(lev, width):
    lo = lev.h - width
    return (lo, lev.h + lev.bx + width), range(lo, lev.h + lev.by + width)


def first_sweep(lev, co, g, out, width):
    (x0, x1), ys = spans(lev, width)

    def body(x, carry):
        xc = x + lev.hc - lev.h
        for y in ys:
            yy = y + ROWS - lev.h
            out[x, y] = co[4][xc, yy : yy + 1, :] * g[x, y]
        return carry

    lax.fori_loop(x0, x1, body, 0)


def sweep(lev, co, g, v, out, width, shift=0):
    (x0, x1), ys = spans(lev, width)

    def body(x, carry):
        def emit(y, here, total, at):
            out[x - shift, y - shift] = KEEP * here + at(co[4]) * (g[x, y] + total)

        row_pass(lev, co, v, x, ys, emit)
        return carry

    lax.fori_loop(x0, x1, body, 0)


def restrict_rows(lev, co, g, v, pair):
    sums = {}
    for dx in (0, 1):
        x = lev.h + 2 * pair + dx

        def emit(y, here, total, at):
            r = g[x, y] + total - at(co[3]) * here
            key = (y - lev.h) // 2
            sums[key] = sums[key] + r if key in sums else r

        row_pass(lev, co, v, x, range(lev.h, lev.h + lev.by), emit)
    return {key: pairsum(t, lev.step, 1) for key, t in sums.items()}


def add_correction(lev, v, corr, out):
    def body(pair, carry):
        for dx in (0, 1):
            x = lev.h + 2 * pair + dx
            for y in range(lev.by):
                out[x, lev.h + y] = v[x, lev.h + y] + corr[pair, y // 2]
        return carry

    lax.fori_loop(0, lev.bx // 2, body, 0)


def coarsen(src, off, bx, by, step, store):
    for x in range(bx // 2):
        t = None
        for dx in (0, 1):
            for dy in (0, 1):
                part = src[off + 2 * x + dx, pl.ds(ROWS + dy, by // 2, stride=2), :]
                t = part if t is None else t + part
        store(x, pairsum(t, step, 1) * 0.25)


class Whole:
    def __init__(self, c, ystep, zstep):
        nx, ny, nl = c.shape
        xi, yi, zi = (iota(c.shape, k) for k in range(3))
        self.ystep, self.zstep = ystep, zstep
        nxt = jnp.concatenate([c[1:], c[-1:]], axis=0)
        self.kx = jnp.where(xi < nx - 1, harmonic(c, nxt), 0.0)
        self.ky = jnp.where(yi < ny - ystep, harmonic(c, roll(c, -ystep, 1)), 0.0)
        self.kz = jnp.where(zi < nl - zstep, harmonic(c, roll(c, -zstep, 2)), 0.0)
        total = jnp.where(xi == nx - 1, c, self.kx) + jnp.where(xi == 0, c, self.back(self.kx))
        total = total + jnp.where(yi >= ny - ystep, c, self.ky)
        total = total + jnp.where(yi < ystep, c, roll(self.ky, ystep, 1))
        total = total + jnp.where(zi >= nl - zstep, c, self.kz)
        total = total + jnp.where(zi < zstep, c, roll(self.kz, zstep, 2))
        self.kk = total
        self.ww = DAMP / total

    def back(self, t):
        return jnp.concatenate([jnp.zeros_like(t[:1]), t[:-1]], axis=0)

    def sums(self, v):
        nxt = jnp.concatenate([v[1:], v[-1:]], axis=0)
        total = self.kx * nxt + self.back(self.kx * v)
        total = total + self.ky * roll(v, -self.ystep, 1) + roll(self.ky * v, self.ystep, 1)
        return total + self.kz * roll(v, -self.zstep, 2) + roll(self.kz * v, self.zstep, 2)

    def sweep(self, v, g):
        return KEEP * v + self.ww * (g + self.sums(v))


def halve(t, zstep):
    nx, ny, nl = t.shape
    t = t.reshape(nx // 2, 2, ny, nl)
    t = t[:, 0] + t[:, 1]
    return pairsum(pairsum(t, 1, 1), zstep, 2)


def double(t):
    nx, ny, nl = t.shape
    return jnp.broadcast_to(t[:, None], (nx, 2, ny, nl)).reshape(2 * nx, ny, nl)


def gather_line(buf, axis, me, count, sems):
    copies = []
    for d in range(1, count[axis]):
        peer = lax.rem(me[axis] + d, count[axis])
        target = (peer, me[1]) if axis == 0 else (me[0], peer)
        piece = buf.at[me[0]] if axis == 0 else buf.at[me[0], me[1]]
        copies.append(
            pltpu.make_async_remote_copy(
                src_ref=piece,
                dst_ref=piece,
                send_sem=sems.at[0, d],
                recv_sem=sems.at[1, d],
                device_id=target,
                device_id_type=MESH,
            )
        )
    for copy in copies:
        copy.start()
    return copies


def finish_line(buf, axis, me, count, sems):
    for d in range(1, count[axis]):
        peer = lax.rem(me[axis] - d + count[axis], count[axis])
        other = lax.rem(me[axis] + d, count[axis])
        target = (other, me[1]) if axis == 0 else (me[0], other)
        mine = buf.at[me[0]] if axis == 0 else buf.at[me[0], me[1]]
        piece = buf.at[peer] if axis == 0 else buf.at[me[0], peer]
        args = dict(
            send_sem=sems.at[0, d], recv_sem=sems.at[1, d], device_id=target, device_id_type=MESH
        )
        pltpu.make_async_remote_copy(src_ref=mine, dst_ref=mine, **args).wait_send()
        pltpu.make_async_remote_copy(src_ref=piece, dst_ref=piece, **args).wait_recv()


def kernel(count, levels, refs_of, table, g_in, labels, out, *scratch):
    r = refs_of(scratch)
    me = (lax.axis_index("gx"), lax.axis_index("gy"))
    axes = (me, count)
    l0, l1, l2 = levels
    bx3, by3 = l2.bx // 2, l2.by // 2

    barrier = pltpu.get_barrier_semaphore()
    greeted = [(d, 0) for d in range(1, count[0])] + [(0, d) for d in range(1, count[1])]
    greeted += [(dx % count[0], dy % count[1]) for dx, dy in DIRS if dx and dy]
    for dx, dy in greeted:
        target = (lax.rem(me[0] + dx, count[0]), lax.rem(me[1] + dy, count[1]))
        pl.semaphore_signal(barrier, inc=1, device_id=target, device_id_type=MESH)

    fetch = pltpu.make_async_copy(
        g_in, r["g0"].at[pl.ds(l0.h, l0.bx), pl.ds(l0.h, l0.by)], r["local"]
    )
    fetch.start()

    c0, c1, c2 = r["c0"], r["c1"], r["c2"]

    def look_up(x, carry):
        lab = labels[x]
        t = jnp.zeros(lab.shape, jnp.float32)
        for klass in range(CLASSES):
            t = jnp.where(lab == klass, table[klass], t)
        c0[l0.hc + x, ROWS : ROWS + l0.by, :] = t
        return carry

    lax.fori_loop(0, l0.bx, look_up, 0)

    def put1(x, t):
        c1[l1.hc + x, ROWS : ROWS + l1.by, :] = t

    def put2(x, t):
        c2[l2.hc + x, ROWS : ROWS + l2.by, :] = t

    def put3(x, t):
        r["c3"][me[0], me[1], x * by3 : (x + 1) * by3, :] = t

    pl.semaphore_wait(barrier, len(greeted))
    e = r["ex"]
    exg0 = exchange(
        g_in, r["g0"], (l0.h,) * 2, (l0.bx, l0.by), (l0.h,) * 2, e.at[0], axes, src_offs=(0, 0)
    )

    def cond_exchange(lev, c, k):
        return exchange(
            c, c, (lev.hc, ROWS), (lev.bx, lev.by), (lev.hc, ROWS), e.at[k], axes
        )

    exc0 = cond_exchange(l0, c0, 1)
    coarsen(c0, l0.hc, l0.bx, l0.by, 1, put1)
    exc1 = cond_exchange(l1, c1, 2)
    coarsen(c1, l1.hc, l1.bx, l1.by, 2, put2)
    exc2 = cond_exchange(l2, c2, 3)
    coarsen(c2, l2.hc, l2.bx, l2.by, 4, put3)
    gather_line(r["c3"], 1, me, count, r["gat"].at[0])

    finish(exc0)
    co0 = [r[n + "0"] for n in ("kx", "ky", "kz", "kk", "ww")]
    co1 = [r[n + "1"] for n in ("kx", "ky", "kz", "kk", "ww")]
    co2 = [r[n + "2"] for n in ("kx", "ky", "kz", "kk", "ww")]
    coefficients(l0, c0, *co0, me, count)
    fetch.wait()
    finish(exg0)

    first_sweep(l0, co0, r["g0"], r["a0"], 2)
    sweep(l0, co0, r["g0"], r["a0"], r["b0"], 1)

    def down(lev, co, g, v, nxt, gn):
        def body(pair, carry):
            for key, t in restrict_rows(lev, co, g, v, pair).items():
                gn[nxt.h + pair, nxt.h + key] = t
            return carry

        lax.fori_loop(0, nxt.bx, body, 0)

    down(l0, co0, r["g0"], r["b0"], l1, r["g1"])

    def field_exchange(lev, f, k):
        return exchange(f, f, (lev.h,) * 2, (lev.bx, lev.by), (lev.h,) * 2, e.at[k], axes)

    exg1 = field_exchange(l1, r["g1"], 4)
    finish_line(r["c3"], 1, me, count, r["gat"].at[0])
    gather_line(r["c3"], 0, me, count, r["gat"].at[1])
    finish(exc1)
    finish(exc2)
    coefficients(l1, c1, *co1, me, count)
    finish(exg1)
    first_sweep(l1, co1, r["g1"], r["a1"], 2)
    sweep(l1, co1, r["g1"], r["a1"], r["b1"], 1)
    down(l1, co1, r["g1"], r["b1"], l2, r["g2"])

    exg2 = field_exchange(l2, r["g2"], 5)
    coefficients(l2, c2, *co2, me, count)
    finish(exg2)
    first_sweep(l2, co2, r["g2"], r["a2"], 3)
    sweep(l2, co2, r["g2"], r["a2"], r["b2"], 2)
    lane8 = iota((8, l2.nz), 1) % 8
    sub8 = iota((8, l2.nz), 0)
    for pair in range(bx3):
        for key, t in restrict_rows(l2, co2, r["g2"], r["b2"], pair).items():
            row = jnp.sum(jnp.where(lane8 == sub8, t, 0.0), axis=0, keepdims=True)
            at = pair * by3 + key
            r["g3"][me[0], me[1], at : at + 1, :] = row
    gather_line(r["g3"], 1, me, count, r["gat"].at[2])
    finish_line(r["c3"], 0, me, count, r["gat"].at[1])
    finish_line(r["g3"], 1, me, count, r["gat"].at[2])
    gather_line(r["g3"], 0, me, count, r["gat"].at[3])

    def assemble(src, dst):
        def body(x, carry):
            for y in range(count[1]):
                for k in range(bx3):
                    dst[x * bx3 + k, y * by3 : (y + 1) * by3, :] = src[
                        x, y, k * by3 : (k + 1) * by3, :
                    ]
            return carry

        lax.fori_loop(0, count[0], body, 0)

    assemble(r["c3"], r["c3w"])
    cond3 = r["c3w"][...]
    w3 = Whole(cond3, 1, 8)
    w4 = Whole(halve(cond3, 8) * 0.25, 2, 16)
    finish_line(r["g3"], 0, me, count, r["gat"].at[3])
    assemble(r["g3"], r["g3w"])
    g3 = r["g3w"][...]
    v3 = w3.ww * g3
    v3 = w3.sweep(v3, g3)
    g4 = halve(g3 + w3.sums(v3) - w3.kk * v3, 8)
    v4 = lax.fori_loop(0, SWEEPS_COARSE - 1, lambda i, v: w4.sweep(v, g4), w4.ww * g4)
    v3 = v3 + double(v4)
    v3 = w3.sweep(v3, g3)
    v3 = w3.sweep(v3, g3)
    r["v3w"][...] = v3

    xmax, ymax = count[0] * bx3 - 1, count[1] * by3 - 1
    for i in range(-1, bx3 + 1):
        x3 = jnp.clip(me[0] * bx3 + i, 0, xmax)
        for j in range(-1, by3 + 1):
            y3 = jnp.clip(me[1] * by3 + j, 0, ymax)
            row = r["v3w"][x3, pl.ds(y3, 1), :]
            t = jnp.where(lane8 == sub8, jnp.broadcast_to(row, (8, l2.nz)), 0.0)
            for step in (1, 2, 4):
                t = pairsum(t, step, 1)
            for dx in (0, 1):
                for dy in (0, 1):
                    x, y = l2.h + 2 * i + dx, l2.h + 2 * j + dy
                    r["p2"][x, y] = r["b2"][x, y] + t
    sweep(l2, co2, r["g2"], r["p2"], r["a2"], 1)
    sweep(l2, co2, r["g2"], r["a2"], r["f2"], 0, shift=l2.h)

    add_correction(l1, r["b1"], r["f2"], r["p1"])
    finish(field_exchange(l1, r["p1"], 6))
    sweep(l1, co1, r["g1"], r["p1"], r["a1"], 1)
    sweep(l1, co1, r["g1"], r["a1"], r["f1"], 0, shift=l1.h)

    add_correction(l0, r["b0"], r["f1"], r["p0"])
    finish(field_exchange(l0, r["p0"], 7))
    sweep(l0, co0, r["g0"], r["p0"], r["a0"], 1)
    sweep(l0, co0, r["g0"], r["a0"], out, 0, shift=l0.h)


def local(count, coil_sources, tissue_labels, class_conductivity):
    _, bx, by, nz = coil_sources.shape
    l0 = Level(0, bx, by, nz, 2, 3)
    l1 = Level(1, bx // 2, by // 2, nz, 2, 3)
    l2 = Level(2, bx // 4, by // 4, nz, 3, 4)
    f32 = jnp.float32
    shapes = {}
    for k, lev in enumerate((l0, l1, l2)):
        for name in ("g", "a", "b", "p"):
            shapes[f"{name}{k}"] = pltpu.VMEM(lev.vshape, f32)
        for name in ("c", "kx", "ky", "kz", "kk", "ww"):
            shapes[f"{name}{k}"] = pltpu.VMEM(lev.cshape, f32)
        if k:
            shapes[f"f{k}"] = pltpu.VMEM((lev.bx, lev.by, 8, nz), f32)
    bx3, by3 = l2.bx // 2, l2.by // 2
    whole = (count[0] * bx3, count[1] * by3, nz)
    for name in ("c3", "g3"):
        shapes[name] = pltpu.VMEM(count + (bx3 * by3, nz), f32)
        shapes[name + "w"] = pltpu.VMEM(whole, f32)
    shapes["v3w"] = pltpu.VMEM(whole, f32)
    shapes["ex"] = pltpu.SemaphoreType.DMA((8, 2, 8))
    shapes["gat"] = pltpu.SemaphoreType.DMA((4, 2, max(count)))
    shapes["local"] = pltpu.SemaphoreType.DMA
    names = list(shapes)

    columns = jnp.transpose(coil_sources, (1, 2, 0, 3))
    result = pl.pallas_call(
        functools.partial(kernel, count, (l0, l1, l2), lambda s: dict(zip(names, s))),
        out_shape=jax.ShapeDtypeStruct(columns.shape, f32),
        in_specs=[
            pl.BlockSpec(memory_space=pltpu.SMEM),
            pl.BlockSpec(memory_space=pl.ANY),
            pl.BlockSpec(memory_space=pltpu.VMEM),
        ],
        out_specs=pl.BlockSpec(memory_space=pltpu.VMEM),
        scratch_shapes=list(shapes.values()),
        compiler_params=pltpu.CompilerParams(
            collective_id=0, has_side_effects=True, vmem_limit_bytes=48 * 2**20
        ),
    )(class_conductivity, columns, tissue_labels)
    return jnp.transpose(result, (2, 0, 1, 3))


def solution(mesh):
    count = (mesh.shape["gx"], mesh.shape["gy"])
    in_specs = (P(None, "gx", "gy", None), P("gx", "gy", None), P())
    out_specs = P(None, "gx", "gy", None)
    return jax.shard_map(
        functools.partial(local, count),
        mesh=mesh,
        in_specs=in_specs,
        out_specs=out_specs,
        check_vma=False,
    )
```

```python
import functools

import jax
import jax.numpy as jnp
from jax import lax
from jax.experimental import pallas as pl
from jax.experimental.pallas import tpu as pltpu
from jax.sharding import PartitionSpec as P

CLASSES = 6
SWEEPS_COARSE = 16
DAMP = 0.8
KEEP = 1.0 - DAMP
MESH = pl.DeviceIdType.MESH
DIRS = [(dx, dy) for dx in (-1, 0, 1) for dy in (-1, 0, 1) if (dx, dy) != (0, 0)]
ROWS = 8


def iota(shape, dim):
    return lax.broadcasted_iota(jnp.int32, shape, dim)


def roll(t, shift, axis):
    return pltpu.roll(t, shift % t.shape[axis], axis)


def pairsum(t, step, axis):
    even = (iota(t.shape, axis) // step) % 2 == 0
    return t + jnp.where(even, roll(t, -step, axis), roll(t, step, axis))


def harmonic(a, b):
    return 2.0 * a * b / (a + b)


class Level:
    def __init__(self, index, bx, by, nz, halo, chalo):
        self.bx, self.by, self.nz = bx, by, nz
        self.h, self.hc, self.step = halo, chalo, 2**index
        self.vshape = (bx + 2 * halo, by + 2 * halo, 8, nz)
        self.cshape = (bx + 2 * chalo, by + 2 * ROWS, nz)


def exchange(src, dst, offs, dims, widths, sems, axes, src_offs=None):
    me, count = axes
    src_offs = offs if src_offs is None else src_offs
    copies = []
    for d, step in enumerate(DIRS):
        s_idx, d_idx = [], []
        for k in (0, 1):
            so, o, n, w = src_offs[k], offs[k], dims[k], widths[k]
            if step[k] == 0:
                s_idx.append(pl.ds(so, n))
                d_idx.append(pl.ds(o, n))
            elif step[k] < 0:
                s_idx.append(pl.ds(so, w))
                d_idx.append(pl.ds(o + n, w))
            else:
                s_idx.append(pl.ds(so + n - w, w))
                d_idx.append(pl.ds(o - w, w))
        target = tuple(lax.rem(me[k] + step[k] + count[k], count[k]) for k in (0, 1))
        copies.append(
            pltpu.make_async_remote_copy(
                src_ref=src.at[tuple(s_idx)],
                dst_ref=dst.at[tuple(d_idx)],
                send_sem=sems.at[0, d],
                recv_sem=sems.at[1, d],
                device_id=target,
                device_id_type=MESH,
            )
        )
    pending = []
    for step, copy in zip(DIRS, copies):
        to = inside(me, count, step)
        pl.when(to)(copy.start)
        pending.append((to, inside(me, count, (-step[0], -step[1])), copy))
    return pending


def inside(me, count, step):
    there = None
    for k in (0, 1):
        if step[k]:
            ok = me[k] > 0 if step[k] < 0 else me[k] < count[k] - 1
            there = ok if there is None else jnp.logical_and(there, ok)
    return there


def finish(pending):
    for to, back, copy in pending:
        pl.when(to)(copy.wait_send)
        pl.when(back)(copy.wait_recv)


def fill(ref, value):
    def body(x, carry):
        ref[x] = jnp.full(ref.shape[1:], value, ref.dtype)
        return carry

    lax.fori_loop(0, ref.shape[0], body, 0)


def clear_halo(lev, ref):
    zero = jnp.zeros(ref.shape[2:], ref.dtype)
    ny = ref.shape[1]

    def edge(k, carry):
        for y in range(ny):
            ref[k, y] = zero
            ref[lev.h + lev.bx + k, y] = zero
        return carry

    lax.fori_loop(0, lev.h, edge, 0)

    def side(x, carry):
        for k in range(lev.h):
            ref[x, k] = zero
            ref[x, lev.h + lev.by + k] = zero
        return carry

    lax.fori_loop(lev.h, lev.h + lev.bx, side, 0)


def coefficients(lev, c, kx, ky, kz, kk, ww, me, count):
    rows = lev.cshape[1]
    shape = (rows, lev.nz)
    ycell = iota(shape, 0) - ROWS + me[1] * lev.by
    ylast = count[1] * lev.by - 1
    zlane = iota(shape, 1)
    zfirst, zlast = zlane < lev.step, zlane >= lev.nz - lev.step
    xlast = count[0] * lev.bx - 1
    xbase = me[0] * lev.bx - lev.hc

    def faces(x, carry):
        cc = c[x]
        cell = x + xbase
        xk = jnp.where(jnp.logical_or(cell == 0, cell == xlast + 1), 0.0, harmonic(cc, c[x - 1]))
        kx[x] = xk
        ky[x] = jnp.where(
            jnp.logical_or(ycell == 0, ycell == ylast + 1), 0.0, harmonic(cc, roll(cc, 1, 0))
        )
        kz[x] = jnp.where(zlast, 0.0, harmonic(cc, roll(cc, -lev.step, 1)))
        return carry

    lax.fori_loop(1, lev.cshape[0], faces, 0)

    def sums(x, carry):
        cc = c[x]
        cell = x + xbase
        yk, zk = ky[x], kz[x]
        total = jnp.where(cell == 0, cc, kx[x]) + jnp.where(cell == xlast, cc, kx[x + 1])
        total = total + jnp.where(ycell == 0, cc, yk) + jnp.where(ycell == ylast, cc, roll(yk, -1, 0))
        total = total + jnp.where(zlast, cc, zk) + jnp.where(zfirst, cc, roll(zk, lev.step, 1))
        kk[x] = total
        ww[x] = DAMP / total
        return carry

    lax.fori_loop(1, lev.cshape[0] - 1, sums, 0)


def row_pass(lev, co, v, x, ys, emit):
    kx, ky, kz, kk, ww = co
    xc = x + lev.hc - lev.h
    held, faces = {}, {}

    def value(y):
        if y not in held:
            held[y] = v[x, y]
        return held[y]

    def at(ref, xx, y):
        yy = y + ROWS - lev.h
        return ref[xx, yy : yy + 1, :]

    def yface(y):
        if y not in faces:
            faces[y] = at(ky, xc, y)
        return faces[y]

    for y in ys:
        here = value(y)
        zk = at(kz, xc, y)
        total = at(kx, xc, y) * v[x - 1, y] + at(kx, xc + 1, y) * v[x + 1, y]
        total = total + yface(y) * value(y - 1) + yface(y + 1) * value(y + 1)
        total = total + zk * roll(here, -lev.step, 1) + roll(zk * here, lev.step, 1)
        emit(y, here, total, functools.partial(at, xx=xc, y=y))


def spans(lev, width):
    lo = lev.h - width
    return (lo, lev.h + lev.bx + width), range(lo, lev.h + lev.by + width)


def pieces(lev, width, part):
    (x0, x1), ys = spans(lev, width)
    if part == "all":
        return [(x0, x1, list(ys))]
    inner = -part[1]
    (i0, i1), iy = spans(lev, inner)
    if part[0] == "inner":
        return [(i0, i1, list(iy))]
    sides = [y for y in ys if y not in iy]
    return [(x0, i0, list(ys)), (i1, x1, list(ys)), (i0, i1, sides)]


def first_sweep(lev, co, g, out, width, part="all"):
    for x0, x1, ys in pieces(lev, width, part):
        first_piece(lev, co, g, out, x0, x1, ys)


def first_piece(lev, co, g, out, x0, x1, ys):
    def body(x, carry):
        xc = x + lev.hc - lev.h
        for y in ys:
            yy = y + ROWS - lev.h
            out[x, y] = co[4][xc, yy : yy + 1, :] * g[x, y]
        return carry

    lax.fori_loop(x0, x1, body, 0)


def sweep(lev, co, g, v, out, width, shift=0, part="all"):
    for x0, x1, ys in pieces(lev, width, part):
        sweep_piece(lev, co, g, v, out, shift, x0, x1, ys)


def sweep_piece(lev, co, g, v, out, shift, x0, x1, ys):
    def body(x, carry):
        def emit(y, here, total, at):
            out[x - shift, y - shift] = KEEP * here + at(co[4]) * (g[x, y] + total)

        row_pass(lev, co, v, x, ys, emit)
        return carry

    lax.fori_loop(x0, x1, body, 0)


def relax_twice(lev, co, g, first, second, pending, width):
    first_sweep(lev, co, g, first, width, part=("inner", 0))
    sweep(lev, co, g, first, second, width - 1, part=("inner", 1))
    finish(pending)
    first_sweep(lev, co, g, first, width, part=("rim", 0))
    sweep(lev, co, g, first, second, width - 1, part=("rim", 1))


def restrict_rows(lev, co, g, v, pair):
    sums = {}
    for dx in (0, 1):
        x = lev.h + 2 * pair + dx

        def emit(y, here, total, at):
            r = g[x, y] + total - at(co[3]) * here
            key = (y - lev.h) // 2
            sums[key] = sums[key] + r if key in sums else r

        row_pass(lev, co, v, x, range(lev.h, lev.h + lev.by), emit)
    return {key: pairsum(t, lev.step, 1) for key, t in sums.items()}


def add_correction(lev, v, corr, out):
    def body(pair, carry):
        for dx in (0, 1):
            x = lev.h + 2 * pair + dx
            for y in range(lev.by):
                out[x, lev.h + y] = v[x, lev.h + y] + corr[pair, y // 2]
        return carry

    lax.fori_loop(0, lev.bx // 2, body, 0)


def coarsen(src, off, bx, by, step, store):
    for x in range(bx // 2):
        t = None
        for dx in (0, 1):
            for dy in (0, 1):
                part = src[off + 2 * x + dx, pl.ds(ROWS + dy, by // 2, stride=2), :]
                t = part if t is None else t + part
        store(x, pairsum(t, step, 1) * 0.25)


class Whole:
    def __init__(self, c, ystep, zstep):
        nx, ny, nl = c.shape
        xi, yi, zi = (iota(c.shape, k) for k in range(3))
        self.ystep, self.zstep = ystep, zstep
        nxt = jnp.concatenate([c[1:], c[-1:]], axis=0)
        self.kx = jnp.where(xi < nx - 1, harmonic(c, nxt), 0.0)
        self.ky = jnp.where(yi < ny - ystep, harmonic(c, roll(c, -ystep, 1)), 0.0)
        self.kz = jnp.where(zi < nl - zstep, harmonic(c, roll(c, -zstep, 2)), 0.0)
        total = jnp.where(xi == nx - 1, c, self.kx) + jnp.where(xi == 0, c, self.back(self.kx))
        total = total + jnp.where(yi >= ny - ystep, c, self.ky)
        total = total + jnp.where(yi < ystep, c, roll(self.ky, ystep, 1))
        total = total + jnp.where(zi >= nl - zstep, c, self.kz)
        total = total + jnp.where(zi < zstep, c, roll(self.kz, zstep, 2))
        self.kk = total
        self.ww = DAMP / total

    def back(self, t):
        return jnp.concatenate([jnp.zeros_like(t[:1]), t[:-1]], axis=0)

    def sums(self, v):
        nxt = jnp.concatenate([v[1:], v[-1:]], axis=0)
        total = self.kx * nxt + self.back(self.kx * v)
        total = total + self.ky * roll(v, -self.ystep, 1) + roll(self.ky * v, self.ystep, 1)
        return total + self.kz * roll(v, -self.zstep, 2) + roll(self.kz * v, self.zstep, 2)

    def sweep(self, v, g):
        return KEEP * v + self.ww * (g + self.sums(v))


def halve(t, zstep):
    nx, ny, nl = t.shape
    t = t.reshape(nx // 2, 2, ny, nl)
    t = t[:, 0] + t[:, 1]
    return pairsum(pairsum(t, 1, 1), zstep, 2)


def double(t):
    nx, ny, nl = t.shape
    return jnp.broadcast_to(t[:, None], (nx, 2, ny, nl)).reshape(2 * nx, ny, nl)


def gather_line(buf, axis, me, count, sems):
    copies = []
    for d in range(1, count[axis]):
        peer = lax.rem(me[axis] + d, count[axis])
        target = (peer, me[1]) if axis == 0 else (me[0], peer)
        piece = buf.at[me[0]] if axis == 0 else buf.at[me[0], me[1]]
        copies.append(
            pltpu.make_async_remote_copy(
                src_ref=piece,
                dst_ref=piece,
                send_sem=sems.at[0, d],
                recv_sem=sems.at[1, d],
                device_id=target,
                device_id_type=MESH,
            )
        )
    for copy in copies:
        copy.start()
    return copies


def finish_line(buf, axis, me, count, sems):
    for d in range(1, count[axis]):
        peer = lax.rem(me[axis] - d + count[axis], count[axis])
        other = lax.rem(me[axis] + d, count[axis])
        target = (other, me[1]) if axis == 0 else (me[0], other)
        mine = buf.at[me[0]] if axis == 0 else buf.at[me[0], me[1]]
        piece = buf.at[peer] if axis == 0 else buf.at[me[0], peer]
        args = dict(
            send_sem=sems.at[0, d], recv_sem=sems.at[1, d], device_id=target, device_id_type=MESH
        )
        pltpu.make_async_remote_copy(src_ref=mine, dst_ref=mine, **args).wait_send()
        pltpu.make_async_remote_copy(src_ref=piece, dst_ref=piece, **args).wait_recv()


def kernel(count, levels, refs_of, table, g_in, labels, out, *scratch):
    r = refs_of(scratch)
    me = (lax.axis_index("gx"), lax.axis_index("gy"))
    axes = (me, count)
    l0, l1, l2 = levels
    bx3, by3 = l2.bx // 2, l2.by // 2

    for k, lev in enumerate(levels):
        fill(r[f"c{k}"], 1.0)
        clear_halo(lev, r[f"g{k}"])
        if k < 2:
            clear_halo(lev, r[f"p{k}"])

    barrier = pltpu.get_barrier_semaphore()
    greeted = [(d, 0) for d in range(1, count[0])] + [(0, d) for d in range(1, count[1])]
    greeted += [(dx % count[0], dy % count[1]) for dx, dy in DIRS if dx and dy]
    for dx, dy in greeted:
        target = (lax.rem(me[0] + dx, count[0]), lax.rem(me[1] + dy, count[1]))
        pl.semaphore_signal(barrier, inc=1, device_id=target, device_id_type=MESH)

    fetch = pltpu.make_async_copy(
        g_in, r["g0"].at[pl.ds(l0.h, l0.bx), pl.ds(l0.h, l0.by)], r["local"]
    )
    fetch.start()

    c0, c1, c2 = r["c0"], r["c1"], r["c2"]

    def look_up(x, carry):
        lab = labels[x]
        t = jnp.zeros(lab.shape, jnp.float32)
        for klass in range(CLASSES):
            t = jnp.where(lab == klass, table[klass], t)
        c0[l0.hc + x, ROWS : ROWS + l0.by, :] = t
        return carry

    lax.fori_loop(0, l0.bx, look_up, 0)

    def put1(x, t):
        c1[l1.hc + x, ROWS : ROWS + l1.by, :] = t

    def put2(x, t):
        c2[l2.hc + x, ROWS : ROWS + l2.by, :] = t

    def put3(x, t):
        r["c3"][me[0], me[1], x * by3 : (x + 1) * by3, :] = t

    pl.semaphore_wait(barrier, len(greeted))
    e = r["ex"]
    def cond_exchange(lev, c, k):
        return exchange(
            c, c, (lev.hc, ROWS), (lev.bx, lev.by), (lev.hc, ROWS), e.at[k], axes
        )

    exc0 = cond_exchange(l0, c0, 1)
    exg0 = exchange(
        g_in, r["g0"], (l0.h,) * 2, (l0.bx, l0.by), (l0.h,) * 2, e.at[0], axes, src_offs=(0, 0)
    )
    coarsen(c0, l0.hc, l0.bx, l0.by, 1, put1)
    exc1 = cond_exchange(l1, c1, 2)
    coarsen(c1, l1.hc, l1.bx, l1.by, 2, put2)
    exc2 = cond_exchange(l2, c2, 3)
    coarsen(c2, l2.hc, l2.bx, l2.by, 4, put3)
    gather_line(r["c3"], 1, me, count, r["gat"].at[0])

    finish(exc0)
    co0 = [r[n + "0"] for n in ("kx", "ky", "kz", "kk", "ww")]
    co1 = [r[n + "1"] for n in ("kx", "ky", "kz", "kk", "ww")]
    co2 = [r[n + "2"] for n in ("kx", "ky", "kz", "kk", "ww")]
    coefficients(l0, c0, *co0, me, count)
    fetch.wait()

    relax_twice(l0, co0, r["g0"], r["a0"], r["b0"], exg0, 2)

    def down(lev, co, g, v, nxt, gn):
        def body(pair, carry):
            for key, t in restrict_rows(lev, co, g, v, pair).items():
                gn[nxt.h + pair, nxt.h + key] = t
            return carry

        lax.fori_loop(0, nxt.bx, body, 0)

    down(l0, co0, r["g0"], r["b0"], l1, r["g1"])

    def field_exchange(lev, f, k):
        return exchange(f, f, (lev.h,) * 2, (lev.bx, lev.by), (lev.h,) * 2, e.at[k], axes)

    exg1 = field_exchange(l1, r["g1"], 4)
    finish_line(r["c3"], 1, me, count, r["gat"].at[0])
    gather_line(r["c3"], 0, me, count, r["gat"].at[1])
    finish(exc1)
    finish(exc2)
    coefficients(l1, c1, *co1, me, count)
    relax_twice(l1, co1, r["g1"], r["a1"], r["b1"], exg1, 2)
    down(l1, co1, r["g1"], r["b1"], l2, r["g2"])

    exg2 = field_exchange(l2, r["g2"], 5)
    coefficients(l2, c2, *co2, me, count)
    finish(exg2)
    first_sweep(l2, co2, r["g2"], r["a2"], 3)
    sweep(l2, co2, r["g2"], r["a2"], r["b2"], 2)
    lane8 = iota((8, l2.nz), 1) % 8
    sub8 = iota((8, l2.nz), 0)
    for pair in range(bx3):
        for key, t in restrict_rows(l2, co2, r["g2"], r["b2"], pair).items():
            row = jnp.sum(jnp.where(lane8 == sub8, t, 0.0), axis=0, keepdims=True)
            at = pair * by3 + key
            r["g3"][me[0], me[1], at : at + 1, :] = row
    gather_line(r["g3"], 1, me, count, r["gat"].at[2])
    finish_line(r["c3"], 0, me, count, r["gat"].at[1])
    finish_line(r["g3"], 1, me, count, r["gat"].at[2])
    gather_line(r["g3"], 0, me, count, r["gat"].at[3])

    def assemble(src, dst):
        def body(x, carry):
            for y in range(count[1]):
                for k in range(bx3):
                    dst[x * bx3 + k, y * by3 : (y + 1) * by3, :] = src[
                        x, y, k * by3 : (k + 1) * by3, :
                    ]
            return carry

        lax.fori_loop(0, count[0], body, 0)

    assemble(r["c3"], r["c3w"])
    cond3 = r["c3w"][...]
    w3 = Whole(cond3, 1, 8)
    w4 = Whole(halve(cond3, 8) * 0.25, 2, 16)
    finish_line(r["g3"], 0, me, count, r["gat"].at[3])
    assemble(r["g3"], r["g3w"])
    g3 = r["g3w"][...]
    v3 = w3.ww * g3
    v3 = w3.sweep(v3, g3)
    g4 = halve(g3 + w3.sums(v3) - w3.kk * v3, 8)
    v4 = lax.fori_loop(0, SWEEPS_COARSE - 1, lambda i, v: w4.sweep(v, g4), w4.ww * g4)
    v3 = v3 + double(v4)
    v3 = w3.sweep(v3, g3)
    v3 = w3.sweep(v3, g3)
    r["v3w"][...] = v3

    xmax, ymax = count[0] * bx3 - 1, count[1] * by3 - 1
    for i in range(-1, bx3 + 1):
        x3 = jnp.clip(me[0] * bx3 + i, 0, xmax)
        for j in range(-1, by3 + 1):
            y3 = jnp.clip(me[1] * by3 + j, 0, ymax)
            row = r["v3w"][x3, pl.ds(y3, 1), :]
            t = jnp.where(lane8 == sub8, jnp.broadcast_to(row, (8, l2.nz)), 0.0)
            for step in (1, 2, 4):
                t = pairsum(t, step, 1)
            for dx in (0, 1):
                for dy in (0, 1):
                    x, y = l2.h + 2 * i + dx, l2.h + 2 * j + dy
                    r["p2"][x, y] = r["b2"][x, y] + t
    sweep(l2, co2, r["g2"], r["p2"], r["a2"], 1)
    sweep(l2, co2, r["g2"], r["a2"], r["f2"], 0, shift=l2.h)

    add_correction(l1, r["b1"], r["f2"], r["p1"])
    exp1 = field_exchange(l1, r["p1"], 6)
    sweep(l1, co1, r["g1"], r["p1"], r["a1"], 1, part=("inner", 1))
    finish(exp1)
    sweep(l1, co1, r["g1"], r["p1"], r["a1"], 1, part=("rim", 1))
    sweep(l1, co1, r["g1"], r["a1"], r["f1"], 0, shift=l1.h)

    add_correction(l0, r["b0"], r["f1"], r["p0"])
    exp0 = field_exchange(l0, r["p0"], 7)
    sweep(l0, co0, r["g0"], r["p0"], r["a0"], 1, part=("inner", 1))
    finish(exp0)
    sweep(l0, co0, r["g0"], r["p0"], r["a0"], 1, part=("rim", 1))
    sweep(l0, co0, r["g0"], r["a0"], out, 0, shift=l0.h)


def local(count, coil_sources, tissue_labels, class_conductivity):
    _, bx, by, nz = coil_sources.shape
    l0 = Level(0, bx, by, nz, 2, 3)
    l1 = Level(1, bx // 2, by // 2, nz, 2, 3)
    l2 = Level(2, bx // 4, by // 4, nz, 3, 4)
    f32 = jnp.float32
    shapes = {}
    for k, lev in enumerate((l0, l1, l2)):
        for name in ("g", "a", "b", "p"):
            shapes[f"{name}{k}"] = pltpu.VMEM(lev.vshape, f32)
        for name in ("c", "kx", "ky", "kz", "kk", "ww"):
            shapes[f"{name}{k}"] = pltpu.VMEM(lev.cshape, f32)
        if k:
            shapes[f"f{k}"] = pltpu.VMEM((lev.bx, lev.by, 8, nz), f32)
    bx3, by3 = l2.bx // 2, l2.by // 2
    whole = (count[0] * bx3, count[1] * by3, nz)
    for name in ("c3", "g3"):
        shapes[name] = pltpu.VMEM(count + (bx3 * by3, nz), f32)
        shapes[name + "w"] = pltpu.VMEM(whole, f32)
    shapes["v3w"] = pltpu.VMEM(whole, f32)
    shapes["ex"] = pltpu.SemaphoreType.DMA((8, 2, 8))
    shapes["gat"] = pltpu.SemaphoreType.DMA((4, 2, max(count)))
    shapes["local"] = pltpu.SemaphoreType.DMA
    names = list(shapes)

    columns = jnp.transpose(coil_sources, (1, 2, 0, 3))
    result = pl.pallas_call(
        functools.partial(kernel, count, (l0, l1, l2), lambda s: dict(zip(names, s))),
        out_shape=jax.ShapeDtypeStruct(columns.shape, f32),
        in_specs=[
            pl.BlockSpec(memory_space=pltpu.SMEM),
            pl.BlockSpec(memory_space=pl.ANY),
            pl.BlockSpec(memory_space=pltpu.VMEM),
        ],
        out_specs=pl.BlockSpec(memory_space=pltpu.VMEM),
        scratch_shapes=list(shapes.values()),
        compiler_params=pltpu.CompilerParams(
            collective_id=0, has_side_effects=True, vmem_limit_bytes=48 * 2**20
        ),
    )(class_conductivity, columns, tissue_labels)
    return jnp.transpose(result, (2, 0, 1, 3))


def solution(mesh):
    count = (mesh.shape["gx"], mesh.shape["gy"])
    in_specs = (P(None, "gx", "gy", None), P("gx", "gy", None), P())
    out_specs = P(None, "gx", "gy", None)
    return jax.shard_map(
        functools.partial(local, count),
        mesh=mesh,
        in_specs=in_specs,
        out_specs=out_specs,
        check_vma=False,
    )
```

```python
import functools

import jax
import jax.numpy as jnp
from jax import lax
from jax.experimental import pallas as pl
from jax.experimental.pallas import tpu as pltpu
from jax.sharding import PartitionSpec as P

CLASSES = 6
SWEEPS_COARSE = 16
DAMP = 0.8
KEEP = 1.0 - DAMP
MESH = pl.DeviceIdType.MESH
DIRS = [(dx, dy) for dx in (-1, 0, 1) for dy in (-1, 0, 1) if (dx, dy) != (0, 0)]
ROWS = 8


def iota(shape, dim):
    return lax.broadcasted_iota(jnp.int32, shape, dim)


def roll(t, shift, axis):
    return pltpu.roll(t, shift % t.shape[axis], axis)


def pairsum(t, step, axis):
    even = (iota(t.shape, axis) // step) % 2 == 0
    return t + jnp.where(even, roll(t, -step, axis), roll(t, step, axis))


def harmonic(a, b):
    return 2.0 * a * b / (a + b)


class Level:
    def __init__(self, index, bx, by, nz, halo, chalo):
        self.bx, self.by, self.nz = bx, by, nz
        self.h, self.hc, self.step = halo, chalo, 2**index
        self.vshape = (bx + 2 * halo, by + 2 * halo, 8, nz)
        self.cshape = (bx + 2 * chalo, by + 2 * ROWS, nz)


def exchange(src, dst, offs, dims, widths, sems, axes, src_offs=None):
    me, count = axes
    src_offs = offs if src_offs is None else src_offs
    copies = []
    for d, step in enumerate(DIRS):
        s_idx, d_idx = [], []
        for k in (0, 1):
            so, o, n, w = src_offs[k], offs[k], dims[k], widths[k]
            if step[k] == 0:
                s_idx.append(pl.ds(so, n))
                d_idx.append(pl.ds(o, n))
            elif step[k] < 0:
                s_idx.append(pl.ds(so, w))
                d_idx.append(pl.ds(o + n, w))
            else:
                s_idx.append(pl.ds(so + n - w, w))
                d_idx.append(pl.ds(o - w, w))
        target = tuple(lax.rem(me[k] + step[k] + count[k], count[k]) for k in (0, 1))
        copies.append(
            pltpu.make_async_remote_copy(
                src_ref=src.at[tuple(s_idx)],
                dst_ref=dst.at[tuple(d_idx)],
                send_sem=sems.at[0, d],
                recv_sem=sems.at[1, d],
                device_id=target,
                device_id_type=MESH,
            )
        )
    pending = []
    for step, copy in zip(DIRS, copies):
        to = inside(me, count, step)
        pl.when(to)(copy.start)
        pending.append((to, inside(me, count, (-step[0], -step[1])), copy))
    return pending


def inside(me, count, step):
    there = None
    for k in (0, 1):
        if step[k]:
            ok = me[k] > 0 if step[k] < 0 else me[k] < count[k] - 1
            there = ok if there is None else jnp.logical_and(there, ok)
    return there


def finish(pending):
    for to, back, copy in pending:
        pl.when(to)(copy.wait_send)
        pl.when(back)(copy.wait_recv)


def fill(ref, value):
    def body(x, carry):
        ref[x] = jnp.full(ref.shape[1:], value, ref.dtype)
        return carry

    lax.fori_loop(0, ref.shape[0], body, 0)


def clear_halo(lev, ref):
    zero = jnp.zeros(ref.shape[2:], ref.dtype)
    ny = ref.shape[1]

    def edge(k, carry):
        for y in range(ny):
            ref[k, y] = zero
            ref[lev.h + lev.bx + k, y] = zero
        return carry

    lax.fori_loop(0, lev.h, edge, 0)

    def side(x, carry):
        for k in range(lev.h):
            ref[x, k] = zero
            ref[x, lev.h + lev.by + k] = zero
        return carry

    lax.fori_loop(lev.h, lev.h + lev.bx, side, 0)


def coefficients(lev, c, kx, ky, kz, kk, ww, me, count):
    rows = lev.cshape[1]
    shape = (rows, lev.nz)
    ycell = iota(shape, 0) - ROWS + me[1] * lev.by
    ylast = count[1] * lev.by - 1
    zlane = iota(shape, 1)
    zfirst, zlast = zlane < lev.step, zlane >= lev.nz - lev.step
    xlast = count[0] * lev.bx - 1
    xbase = me[0] * lev.bx - lev.hc

    def faces(x, carry):
        cc = c[x]
        cell = x + xbase
        xk = jnp.where(jnp.logical_or(cell == 0, cell == xlast + 1), 0.0, harmonic(cc, c[x - 1]))
        kx[x] = xk
        ky[x] = jnp.where(
            jnp.logical_or(ycell == 0, ycell == ylast + 1), 0.0, harmonic(cc, roll(cc, 1, 0))
        )
        kz[x] = jnp.where(zlast, 0.0, harmonic(cc, roll(cc, -lev.step, 1)))
        return carry

    lax.fori_loop(1, lev.cshape[0], faces, 0)

    def sums(x, carry):
        cc = c[x]
        cell = x + xbase
        yk, zk = ky[x], kz[x]
        total = jnp.where(cell == 0, cc, kx[x]) + jnp.where(cell == xlast, cc, kx[x + 1])
        total = total + jnp.where(ycell == 0, cc, yk) + jnp.where(ycell == ylast, cc, roll(yk, -1, 0))
        total = total + jnp.where(zlast, cc, zk) + jnp.where(zfirst, cc, roll(zk, lev.step, 1))
        kk[x] = total
        ww[x] = DAMP / total
        return carry

    lax.fori_loop(1, lev.cshape[0] - 1, sums, 0)


def row_pass(lev, co, v, x, ys, emit):
    kx, ky, kz, kk, ww = co
    xc = x + lev.hc - lev.h
    held, faces = {}, {}

    def value(y):
        if y not in held:
            held[y] = v[x, y]
        return held[y]

    def at(ref, xx, y):
        yy = y + ROWS - lev.h
        return ref[xx, yy : yy + 1, :]

    def yface(y):
        if y not in faces:
            faces[y] = at(ky, xc, y)
        return faces[y]

    for y in ys:
        here = value(y)
        zk = at(kz, xc, y)
        total = at(kx, xc, y) * v[x - 1, y] + at(kx, xc + 1, y) * v[x + 1, y]
        total = total + yface(y) * value(y - 1) + yface(y + 1) * value(y + 1)
        total = total + zk * roll(here, -lev.step, 1) + roll(zk * here, lev.step, 1)
        emit(y, here, total, functools.partial(at, xx=xc, y=y))


def spans(lev, width):
    lo = lev.h - width
    return (lo, lev.h + lev.bx + width), range(lo, lev.h + lev.by + width)


def pieces(lev, width, part):
    (x0, x1), ys = spans(lev, width)
    if part == "all":
        return [(x0, x1, list(ys))]
    inner = -part[1]
    (i0, i1), iy = spans(lev, inner)
    if part[0] == "inner":
        return [(i0, i1, list(iy))]
    sides = [y for y in ys if y not in iy]
    return [(x0, i0, list(ys)), (i1, x1, list(ys)), (i0, i1, sides)]


def first_sweep(lev, co, g, out, width, part="all"):
    for x0, x1, ys in pieces(lev, width, part):
        first_piece(lev, co, g, out, x0, x1, ys)


def first_piece(lev, co, g, out, x0, x1, ys):
    def body(x, carry):
        xc = x + lev.hc - lev.h
        for y in ys:
            yy = y + ROWS - lev.h
            out[x, y] = co[4][xc, yy : yy + 1, :] * g[x, y]
        return carry

    lax.fori_loop(x0, x1, body, 0)


def sweep(lev, co, g, v, out, width, shift=0, part="all"):
    for x0, x1, ys in pieces(lev, width, part):
        sweep_piece(lev, co, g, v, out, shift, x0, x1, ys)


def sweep_piece(lev, co, g, v, out, shift, x0, x1, ys):
    def body(x, carry):
        def emit(y, here, total, at):
            out[x - shift, y - shift] = KEEP * here + at(co[4]) * (g[x, y] + total)

        row_pass(lev, co, v, x, ys, emit)
        return carry

    lax.fori_loop(x0, x1, body, 0)


def relax_twice(lev, co, g, first, second, pending, width):
    first_sweep(lev, co, g, first, width, part=("inner", 0))
    sweep(lev, co, g, first, second, width - 1, part=("inner", 1))
    finish(pending)
    first_sweep(lev, co, g, first, width, part=("rim", 0))
    sweep(lev, co, g, first, second, width - 1, part=("rim", 1))


def restrict_rows(lev, co, g, v, pair):
    sums = {}
    for dx in (0, 1):
        x = lev.h + 2 * pair + dx

        def emit(y, here, total, at):
            r = g[x, y] + total - at(co[3]) * here
            key = (y - lev.h) // 2
            sums[key] = sums[key] + r if key in sums else r

        row_pass(lev, co, v, x, range(lev.h, lev.h + lev.by), emit)
    return {key: pairsum(t, lev.step, 1) for key, t in sums.items()}


def add_correction(lev, v, corr, out):
    def body(pair, carry):
        for dx in (0, 1):
            x = lev.h + 2 * pair + dx
            for y in range(lev.by):
                out[x, lev.h + y] = v[x, lev.h + y] + corr[1 + pair, 1 + y // 2]
        return carry

    lax.fori_loop(0, lev.bx // 2, body, 0)


def add_halo(lev, corr, out):
    nx, ny = lev.bx // 2 + 2, lev.by // 2 + 2

    def grow(x, ys):
        for y in ys:
            for dx in (0, 1):
                for dy in (0, 1):
                    at = (2 * x + dx, 2 * y + dy)
                    out[at] = out[at] + corr[x, y]

    grow(0, range(ny))
    grow(nx - 1, range(ny))

    def body(x, carry):
        grow(x, (0, ny - 1))
        return carry

    lax.fori_loop(1, nx - 1, body, 0)


def coarsen(src, off, bx, by, step, store):
    for x in range(bx // 2):
        t = None
        for dx in (0, 1):
            for dy in (0, 1):
                part = src[off + 2 * x + dx, pl.ds(ROWS + dy, by // 2, stride=2), :]
                t = part if t is None else t + part
        store(x, pairsum(t, step, 1) * 0.25)


class Whole:
    def __init__(self, c, ystep, zstep):
        nx, ny, nl = c.shape
        xi, yi, zi = (iota(c.shape, k) for k in range(3))
        self.ystep, self.zstep = ystep, zstep
        nxt = jnp.concatenate([c[1:], c[-1:]], axis=0)
        self.kx = jnp.where(xi < nx - 1, harmonic(c, nxt), 0.0)
        self.ky = jnp.where(yi < ny - ystep, harmonic(c, roll(c, -ystep, 1)), 0.0)
        self.kz = jnp.where(zi < nl - zstep, harmonic(c, roll(c, -zstep, 2)), 0.0)
        total = jnp.where(xi == nx - 1, c, self.kx) + jnp.where(xi == 0, c, self.back(self.kx))
        total = total + jnp.where(yi >= ny - ystep, c, self.ky)
        total = total + jnp.where(yi < ystep, c, roll(self.ky, ystep, 1))
        total = total + jnp.where(zi >= nl - zstep, c, self.kz)
        total = total + jnp.where(zi < zstep, c, roll(self.kz, zstep, 2))
        self.kk = total
        self.ww = DAMP / total

    def back(self, t):
        return jnp.concatenate([jnp.zeros_like(t[:1]), t[:-1]], axis=0)

    def sums(self, v):
        nxt = jnp.concatenate([v[1:], v[-1:]], axis=0)
        total = self.kx * nxt + self.back(self.kx * v)
        total = total + self.ky * roll(v, -self.ystep, 1) + roll(self.ky * v, self.ystep, 1)
        return total + self.kz * roll(v, -self.zstep, 2) + roll(self.kz * v, self.zstep, 2)

    def sweep(self, v, g):
        return KEEP * v + self.ww * (g + self.sums(v))


def halve(t, zstep):
    nx, ny, nl = t.shape
    t = t.reshape(nx // 2, 2, ny, nl)
    t = t[:, 0] + t[:, 1]
    return pairsum(pairsum(t, 1, 1), zstep, 2)


def double(t):
    nx, ny, nl = t.shape
    return jnp.broadcast_to(t[:, None], (nx, 2, ny, nl)).reshape(2 * nx, ny, nl)


def gather_line(buf, axis, me, count, sems):
    copies = []
    for d in range(1, count[axis]):
        peer = lax.rem(me[axis] + d, count[axis])
        target = (peer, me[1]) if axis == 0 else (me[0], peer)
        piece = buf.at[me[0]] if axis == 0 else buf.at[me[0], me[1]]
        copies.append(
            pltpu.make_async_remote_copy(
                src_ref=piece,
                dst_ref=piece,
                send_sem=sems.at[0, d],
                recv_sem=sems.at[1, d],
                device_id=target,
                device_id_type=MESH,
            )
        )
    for copy in copies:
        copy.start()
    return copies


def finish_line(buf, axis, me, count, sems):
    for d in range(1, count[axis]):
        peer = lax.rem(me[axis] - d + count[axis], count[axis])
        other = lax.rem(me[axis] + d, count[axis])
        target = (other, me[1]) if axis == 0 else (me[0], other)
        mine = buf.at[me[0]] if axis == 0 else buf.at[me[0], me[1]]
        piece = buf.at[peer] if axis == 0 else buf.at[me[0], peer]
        args = dict(
            send_sem=sems.at[0, d], recv_sem=sems.at[1, d], device_id=target, device_id_type=MESH
        )
        pltpu.make_async_remote_copy(src_ref=mine, dst_ref=mine, **args).wait_send()
        pltpu.make_async_remote_copy(src_ref=piece, dst_ref=piece, **args).wait_recv()


def kernel(count, levels, refs_of, table, g_in, labels, out, *scratch):
    r = refs_of(scratch)
    me = (lax.axis_index("gx"), lax.axis_index("gy"))
    axes = (me, count)
    l0, l1, l2 = levels
    bx3, by3 = l2.bx // 2, l2.by // 2

    for k, lev in enumerate(levels):
        fill(r[f"c{k}"], 1.0)
        clear_halo(lev, r[f"g{k}"])
        if k < 2:
            clear_halo(lev, r[f"p{k}"])
            fill(r[f"f{k + 1}"], 0.0)

    barrier = pltpu.get_barrier_semaphore()
    greeted = [(d, 0) for d in range(1, count[0])] + [(0, d) for d in range(1, count[1])]
    greeted += [(dx % count[0], dy % count[1]) for dx, dy in DIRS if dx and dy]
    for dx, dy in greeted:
        target = (lax.rem(me[0] + dx, count[0]), lax.rem(me[1] + dy, count[1]))
        pl.semaphore_signal(barrier, inc=1, device_id=target, device_id_type=MESH)

    fetch = pltpu.make_async_copy(
        g_in, r["g0"].at[pl.ds(l0.h, l0.bx), pl.ds(l0.h, l0.by)], r["local"]
    )
    fetch.start()

    c0, c1, c2 = r["c0"], r["c1"], r["c2"]

    def look_up(x, carry):
        lab = labels[x]
        t = jnp.zeros(lab.shape, jnp.float32)
        for klass in range(CLASSES):
            t = jnp.where(lab == klass, table[klass], t)
        c0[l0.hc + x, ROWS : ROWS + l0.by, :] = t
        return carry

    lax.fori_loop(0, l0.bx, look_up, 0)

    def put1(x, t):
        c1[l1.hc + x, ROWS : ROWS + l1.by, :] = t

    def put2(x, t):
        c2[l2.hc + x, ROWS : ROWS + l2.by, :] = t

    def put3(x, t):
        r["c3"][me[0], me[1], x * by3 : (x + 1) * by3, :] = t

    pl.semaphore_wait(barrier, len(greeted))
    e = r["ex"]
    def cond_exchange(lev, c, k):
        return exchange(
            c, c, (lev.hc, ROWS), (lev.bx, lev.by), (lev.hc, ROWS), e.at[k], axes
        )

    exc0 = cond_exchange(l0, c0, 1)
    exg0 = exchange(
        g_in, r["g0"], (l0.h,) * 2, (l0.bx, l0.by), (l0.h,) * 2, e.at[0], axes, src_offs=(0, 0)
    )
    coarsen(c0, l0.hc, l0.bx, l0.by, 1, put1)
    exc1 = cond_exchange(l1, c1, 2)
    coarsen(c1, l1.hc, l1.bx, l1.by, 2, put2)
    exc2 = cond_exchange(l2, c2, 3)
    coarsen(c2, l2.hc, l2.bx, l2.by, 4, put3)
    gather_line(r["c3"], 1, me, count, r["gat"].at[0])

    finish(exc0)
    co0 = [r[n + "0"] for n in ("kx", "ky", "kz", "kk", "ww")]
    co1 = [r[n + "1"] for n in ("kx", "ky", "kz", "kk", "ww")]
    co2 = [r[n + "2"] for n in ("kx", "ky", "kz", "kk", "ww")]
    coefficients(l0, c0, *co0, me, count)
    fetch.wait()

    relax_twice(l0, co0, r["g0"], r["a0"], r["b0"], exg0, 2)

    def down(lev, co, g, v, nxt, gn):
        def body(pair, carry):
            for key, t in restrict_rows(lev, co, g, v, pair).items():
                gn[nxt.h + pair, nxt.h + key] = t
            return carry

        lax.fori_loop(0, nxt.bx, body, 0)

    down(l0, co0, r["g0"], r["b0"], l1, r["g1"])

    def field_exchange(lev, f, k, to=None):
        to = f if to is None else to
        return exchange(f, to, (lev.h,) * 2, (lev.bx, lev.by), (lev.h,) * 2, e.at[k], axes)

    def correction_exchange(lev, f, k):
        return exchange(f, f, (1, 1), (lev.bx, lev.by), (1, 1), e.at[k], axes)

    exg1 = field_exchange(l1, r["g1"], 4)
    exp0 = field_exchange(l0, r["b0"], 7, r["p0"])
    finish_line(r["c3"], 1, me, count, r["gat"].at[0])
    gather_line(r["c3"], 0, me, count, r["gat"].at[1])
    finish(exc1)
    finish(exc2)
    coefficients(l1, c1, *co1, me, count)
    relax_twice(l1, co1, r["g1"], r["a1"], r["b1"], exg1, 2)
    down(l1, co1, r["g1"], r["b1"], l2, r["g2"])

    exg2 = field_exchange(l2, r["g2"], 5)
    exp1 = field_exchange(l1, r["b1"], 6, r["p1"])
    coefficients(l2, c2, *co2, me, count)
    finish(exg2)
    first_sweep(l2, co2, r["g2"], r["a2"], 3)
    sweep(l2, co2, r["g2"], r["a2"], r["b2"], 2)
    lane8 = iota((8, l2.nz), 1) % 8
    sub8 = iota((8, l2.nz), 0)
    for pair in range(bx3):
        for key, t in restrict_rows(l2, co2, r["g2"], r["b2"], pair).items():
            row = jnp.sum(jnp.where(lane8 == sub8, t, 0.0), axis=0, keepdims=True)
            at = pair * by3 + key
            r["g3"][me[0], me[1], at : at + 1, :] = row
    gather_line(r["g3"], 1, me, count, r["gat"].at[2])
    finish_line(r["c3"], 0, me, count, r["gat"].at[1])
    finish_line(r["g3"], 1, me, count, r["gat"].at[2])
    gather_line(r["g3"], 0, me, count, r["gat"].at[3])

    def assemble(src, dst):
        def body(x, carry):
            for y in range(count[1]):
                for k in range(bx3):
                    dst[x * bx3 + k, y * by3 : (y + 1) * by3, :] = src[
                        x, y, k * by3 : (k + 1) * by3, :
                    ]
            return carry

        lax.fori_loop(0, count[0], body, 0)

    assemble(r["c3"], r["c3w"])
    cond3 = r["c3w"][...]
    w3 = Whole(cond3, 1, 8)
    w4 = Whole(halve(cond3, 8) * 0.25, 2, 16)
    finish_line(r["g3"], 0, me, count, r["gat"].at[3])
    assemble(r["g3"], r["g3w"])
    g3 = r["g3w"][...]
    v3 = w3.ww * g3
    v3 = w3.sweep(v3, g3)
    g4 = halve(g3 + w3.sums(v3) - w3.kk * v3, 8)
    v4 = lax.fori_loop(0, SWEEPS_COARSE - 1, lambda i, v: w4.sweep(v, g4), w4.ww * g4)
    v3 = v3 + double(v4)
    v3 = w3.sweep(v3, g3)
    v3 = w3.sweep(v3, g3)
    r["v3w"][...] = v3

    xmax, ymax = count[0] * bx3 - 1, count[1] * by3 - 1
    for i in range(-1, bx3 + 1):
        x3 = jnp.clip(me[0] * bx3 + i, 0, xmax)
        for j in range(-1, by3 + 1):
            y3 = jnp.clip(me[1] * by3 + j, 0, ymax)
            row = r["v3w"][x3, pl.ds(y3, 1), :]
            t = jnp.where(lane8 == sub8, jnp.broadcast_to(row, (8, l2.nz)), 0.0)
            for step in (1, 2, 4):
                t = pairsum(t, step, 1)
            for dx in (0, 1):
                for dy in (0, 1):
                    x, y = l2.h + 2 * i + dx, l2.h + 2 * j + dy
                    r["p2"][x, y] = r["b2"][x, y] + t
    sweep(l2, co2, r["g2"], r["p2"], r["a2"], 1)
    sweep(l2, co2, r["g2"], r["a2"], r["f2"], 0, shift=l2.h - 1)

    exf2 = correction_exchange(l2, r["f2"], 9)
    add_correction(l1, r["b1"], r["f2"], r["p1"])
    sweep(l1, co1, r["g1"], r["p1"], r["a1"], 1, part=("inner", 1))
    finish(exp1)
    finish(exf2)
    add_halo(l1, r["f2"], r["p1"])
    sweep(l1, co1, r["g1"], r["p1"], r["a1"], 1, part=("rim", 1))
    sweep(l1, co1, r["g1"], r["a1"], r["f1"], 0, shift=l1.h - 1)

    exf1 = correction_exchange(l1, r["f1"], 8)
    add_correction(l0, r["b0"], r["f1"], r["p0"])
    sweep(l0, co0, r["g0"], r["p0"], r["a0"], 1, part=("inner", 1))
    finish(exp0)
    finish(exf1)
    add_halo(l0, r["f1"], r["p0"])
    sweep(l0, co0, r["g0"], r["p0"], r["a0"], 1, part=("rim", 1))
    sweep(l0, co0, r["g0"], r["a0"], out, 0, shift=l0.h)


def local(count, coil_sources, tissue_labels, class_conductivity):
    _, bx, by, nz = coil_sources.shape
    l0 = Level(0, bx, by, nz, 2, 3)
    l1 = Level(1, bx // 2, by // 2, nz, 2, 3)
    l2 = Level(2, bx // 4, by // 4, nz, 3, 4)
    f32 = jnp.float32
    shapes = {}
    for k, lev in enumerate((l0, l1, l2)):
        for name in ("g", "a", "b", "p"):
            shapes[f"{name}{k}"] = pltpu.VMEM(lev.vshape, f32)
        for name in ("c", "kx", "ky", "kz", "kk", "ww"):
            shapes[f"{name}{k}"] = pltpu.VMEM(lev.cshape, f32)
        if k:
            shapes[f"f{k}"] = pltpu.VMEM((lev.bx + 2, lev.by + 2, 8, nz), f32)
    bx3, by3 = l2.bx // 2, l2.by // 2
    whole = (count[0] * bx3, count[1] * by3, nz)
    for name in ("c3", "g3"):
        shapes[name] = pltpu.VMEM(count + (bx3 * by3, nz), f32)
        shapes[name + "w"] = pltpu.VMEM(whole, f32)
    shapes["v3w"] = pltpu.VMEM(whole, f32)
    shapes["ex"] = pltpu.SemaphoreType.DMA((10, 2, 8))
    shapes["gat"] = pltpu.SemaphoreType.DMA((4, 2, max(count)))
    shapes["local"] = pltpu.SemaphoreType.DMA
    names = list(shapes)

    columns = jnp.transpose(coil_sources, (1, 2, 0, 3))
    result = pl.pallas_call(
        functools.partial(kernel, count, (l0, l1, l2), lambda s: dict(zip(names, s))),
        out_shape=jax.ShapeDtypeStruct(columns.shape, f32),
        in_specs=[
            pl.BlockSpec(memory_space=pltpu.SMEM),
            pl.BlockSpec(memory_space=pl.ANY),
            pl.BlockSpec(memory_space=pltpu.VMEM),
        ],
        out_specs=pl.BlockSpec(memory_space=pltpu.VMEM),
        scratch_shapes=list(shapes.values()),
        compiler_params=pltpu.CompilerParams(
            collective_id=0, has_side_effects=True, vmem_limit_bytes=48 * 2**20
        ),
    )(class_conductivity, columns, tissue_labels)
    return jnp.transpose(result, (2, 0, 1, 3))


def solution(mesh):
    count = (mesh.shape["gx"], mesh.shape["gy"])
    in_specs = (P(None, "gx", "gy", None), P("gx", "gy", None), P())
    out_specs = P(None, "gx", "gy", None)
    return jax.shard_map(
        functools.partial(local, count),
        mesh=mesh,
        in_specs=in_specs,
        out_specs=out_specs,
        check_vma=False,
    )
```

```python
import functools

import jax
import jax.numpy as jnp
from jax import lax
from jax.experimental import pallas as pl
from jax.experimental.pallas import tpu as pltpu
from jax.sharding import PartitionSpec as P

CLASSES = 6
SWEEPS_COARSE = 16
DAMP = 0.8
KEEP = 1.0 - DAMP
MESH = pl.DeviceIdType.MESH
DIRS = [(dx, dy) for dx in (-1, 0, 1) for dy in (-1, 0, 1) if (dx, dy) != (0, 0)]
ROWS = 8


def iota(shape, dim):
    return lax.broadcasted_iota(jnp.int32, shape, dim)


def roll(t, shift, axis):
    return pltpu.roll(t, shift % t.shape[axis], axis)


def pairsum(t, step, axis):
    even = (iota(t.shape, axis) // step) % 2 == 0
    return t + jnp.where(even, roll(t, -step, axis), roll(t, step, axis))


def harmonic(a, b):
    return 2.0 * a * b / (a + b)


class Level:
    def __init__(self, index, bx, by, nz, halo, chalo):
        self.bx, self.by, self.nz = bx, by, nz
        self.h, self.hc, self.step = halo, chalo, 2**index
        self.vshape = (bx + 2 * halo, by + 2 * halo, 8, nz)
        self.cshape = (bx + 2 * chalo, by + 2 * ROWS, nz)


def exchange(src, dst, offs, dims, widths, sems, axes, src_offs=None):
    me, count = axes
    src_offs = offs if src_offs is None else src_offs
    copies = []
    for d, step in enumerate(DIRS):
        s_idx, d_idx = [], []
        for k in (0, 1):
            so, o, n, w = src_offs[k], offs[k], dims[k], widths[k]
            if step[k] == 0:
                s_idx.append(pl.ds(so, n))
                d_idx.append(pl.ds(o, n))
            elif step[k] < 0:
                s_idx.append(pl.ds(so, w))
                d_idx.append(pl.ds(o + n, w))
            else:
                s_idx.append(pl.ds(so + n - w, w))
                d_idx.append(pl.ds(o - w, w))
        target = tuple(lax.rem(me[k] + step[k] + count[k], count[k]) for k in (0, 1))
        copies.append(
            pltpu.make_async_remote_copy(
                src_ref=src.at[tuple(s_idx)],
                dst_ref=dst.at[tuple(d_idx)],
                send_sem=sems.at[0, d],
                recv_sem=sems.at[1, d],
                device_id=target,
                device_id_type=MESH,
            )
        )
    pending = []
    for step, copy in zip(DIRS, copies):
        to = inside(me, count, step)
        pl.when(to)(copy.start)
        pending.append((to, inside(me, count, (-step[0], -step[1])), copy))
    return pending


def inside(me, count, step):
    there = None
    for k in (0, 1):
        if step[k]:
            ok = me[k] > 0 if step[k] < 0 else me[k] < count[k] - 1
            there = ok if there is None else jnp.logical_and(there, ok)
    return there


def finish(pending):
    for to, back, copy in pending:
        pl.when(to)(copy.wait_send)
        pl.when(back)(copy.wait_recv)


def fill(ref, value):
    def body(x, carry):
        ref[x] = jnp.full(ref.shape[1:], value, ref.dtype)
        return carry

    lax.fori_loop(0, ref.shape[0], body, 0)


def clear_halo(lev, ref):
    zero = jnp.zeros(ref.shape[2:], ref.dtype)
    ny = ref.shape[1]

    def edge(k, carry):
        for y in range(ny):
            ref[k, y] = zero
            ref[lev.h + lev.bx + k, y] = zero
        return carry

    lax.fori_loop(0, lev.h, edge, 0)

    def side(x, carry):
        for k in range(lev.h):
            ref[x, k] = zero
            ref[x, lev.h + lev.by + k] = zero
        return carry

    lax.fori_loop(lev.h, lev.h + lev.bx, side, 0)


def coefficients(lev, c, kx, ky, kz, kk, ww, me, count):
    rows = lev.cshape[1]
    shape = (rows, lev.nz)
    ycell = iota(shape, 0) - ROWS + me[1] * lev.by
    ylast = count[1] * lev.by - 1
    zlane = iota(shape, 1)
    zfirst, zlast = zlane < lev.step, zlane >= lev.nz - lev.step
    xlast = count[0] * lev.bx - 1
    xbase = me[0] * lev.bx - lev.hc

    def faces(x, carry):
        cc = c[x]
        cell = x + xbase
        xk = jnp.where(jnp.logical_or(cell == 0, cell == xlast + 1), 0.0, harmonic(cc, c[x - 1]))
        kx[x] = xk
        ky[x] = jnp.where(
            jnp.logical_or(ycell == 0, ycell == ylast + 1), 0.0, harmonic(cc, roll(cc, 1, 0))
        )
        kz[x] = jnp.where(zlast, 0.0, harmonic(cc, roll(cc, -lev.step, 1)))
        return carry

    lax.fori_loop(1, lev.cshape[0], faces, 0)

    def sums(x, carry):
        cc = c[x]
        cell = x + xbase
        yk, zk = ky[x], kz[x]
        total = jnp.where(cell == 0, cc, kx[x]) + jnp.where(cell == xlast, cc, kx[x + 1])
        total = total + jnp.where(ycell == 0, cc, yk) + jnp.where(ycell == ylast, cc, roll(yk, -1, 0))
        total = total + jnp.where(zlast, cc, zk) + jnp.where(zfirst, cc, roll(zk, lev.step, 1))
        kk[x] = total
        ww[x] = DAMP / total
        return carry

    lax.fori_loop(1, lev.cshape[0] - 1, sums, 0)


def row_pass(lev, co, v, x, ys, emit):
    kx, ky, kz, kk, ww = co
    xc = x + lev.hc - lev.h
    held, faces = {}, {}

    def value(y):
        if y not in held:
            held[y] = v[x, y]
        return held[y]

    def at(ref, xx, y):
        yy = y + ROWS - lev.h
        return ref[xx, yy : yy + 1, :]

    def yface(y):
        if y not in faces:
            faces[y] = at(ky, xc, y)
        return faces[y]

    for y in ys:
        here = value(y)
        zk = at(kz, xc, y)
        total = at(kx, xc, y) * v[x - 1, y] + at(kx, xc + 1, y) * v[x + 1, y]
        total = total + yface(y) * value(y - 1) + yface(y + 1) * value(y + 1)
        total = total + zk * roll(here, -lev.step, 1) + roll(zk * here, lev.step, 1)
        emit(y, here, total, functools.partial(at, xx=xc, y=y))


def spans(lev, width):
    lo = lev.h - width
    return (lo, lev.h + lev.bx + width), range(lo, lev.h + lev.by + width)


def pieces(lev, width, part):
    (x0, x1), ys = spans(lev, width)
    if part == "all":
        return [(x0, x1, list(ys))]
    inner = -part[1]
    (i0, i1), iy = spans(lev, inner)
    if part[0] == "inner":
        return [(i0, i1, list(iy))]
    sides = [y for y in ys if y not in iy]
    return [(x0, i0, list(ys)), (i1, x1, list(ys)), (i0, i1, sides)]


def first_sweep(lev, co, g, out, width, part="all"):
    for x0, x1, ys in pieces(lev, width, part):
        first_piece(lev, co, g, out, x0, x1, ys)


def first_piece(lev, co, g, out, x0, x1, ys):
    def body(x, carry):
        xc = x + lev.hc - lev.h
        for y in ys:
            yy = y + ROWS - lev.h
            out[x, y] = co[4][xc, yy : yy + 1, :] * g[x, y]
        return carry

    lax.fori_loop(x0, x1, body, 0)


def sweep(lev, co, g, v, out, width, shift=0, part="all"):
    for x0, x1, ys in pieces(lev, width, part):
        sweep_piece(lev, co, g, v, out, shift, x0, x1, ys)


def sweep_piece(lev, co, g, v, out, shift, x0, x1, ys):
    def body(x, carry):
        def emit(y, here, total, at):
            out[x - shift, y - shift] = KEEP * here + at(co[4]) * (g[x, y] + total)

        row_pass(lev, co, v, x, ys, emit)
        return carry

    lax.fori_loop(x0, x1, body, 0)


def relax_twice(lev, co, g, first, second, pending, width):
    first_sweep(lev, co, g, first, width, part=("inner", 0))
    sweep(lev, co, g, first, second, width - 1, part=("inner", 1))
    finish(pending)
    first_sweep(lev, co, g, first, width, part=("rim", 0))
    sweep(lev, co, g, first, second, width - 1, part=("rim", 1))


def restrict_rows(lev, co, g, v, pair):
    sums = {}
    for dx in (0, 1):
        x = lev.h + 2 * pair + dx

        def emit(y, here, total, at):
            r = g[x, y] + total - at(co[3]) * here
            key = (y - lev.h) // 2
            sums[key] = sums[key] + r if key in sums else r

        row_pass(lev, co, v, x, range(lev.h, lev.h + lev.by), emit)
    return {key: pairsum(t, lev.step, 1) for key, t in sums.items()}


def add_correction(lev, v, corr, out):
    def body(pair, carry):
        for dx in (0, 1):
            x = lev.h + 2 * pair + dx
            for y in range(lev.by):
                out[x, lev.h + y] = v[x, lev.h + y] + corr[1 + pair, 1 + y // 2]
        return carry

    lax.fori_loop(0, lev.bx // 2, body, 0)


def add_halo(lev, corr, out):
    nx, ny = lev.bx // 2 + 2, lev.by // 2 + 2

    def grow(x, ys):
        for y in ys:
            for dx in (0, 1):
                for dy in (0, 1):
                    at = (2 * x + dx, 2 * y + dy)
                    out[at] = out[at] + corr[x, y]

    grow(0, range(ny))
    grow(nx - 1, range(ny))

    def body(x, carry):
        grow(x, (0, ny - 1))
        return carry

    lax.fori_loop(1, nx - 1, body, 0)


def coarsen(src, off, bx, by, step, store):
    for x in range(bx // 2):
        t = None
        for dx in (0, 1):
            for dy in (0, 1):
                part = src[off + 2 * x + dx, pl.ds(ROWS + dy, by // 2, stride=2), :]
                t = part if t is None else t + part
        store(x, pairsum(t, step, 1) * 0.25)


class Whole:
    def __init__(self, c, ystep, zstep):
        nx, ny, nl = c.shape
        xi, yi, zi = (iota(c.shape, k) for k in range(3))
        self.ystep, self.zstep = ystep, zstep
        nxt = jnp.concatenate([c[1:], c[-1:]], axis=0)
        self.kx = jnp.where(xi < nx - 1, harmonic(c, nxt), 0.0)
        self.ky = jnp.where(yi < ny - ystep, harmonic(c, roll(c, -ystep, 1)), 0.0)
        self.kz = jnp.where(zi < nl - zstep, harmonic(c, roll(c, -zstep, 2)), 0.0)
        total = jnp.where(xi == nx - 1, c, self.kx) + jnp.where(xi == 0, c, self.back(self.kx))
        total = total + jnp.where(yi >= ny - ystep, c, self.ky)
        total = total + jnp.where(yi < ystep, c, roll(self.ky, ystep, 1))
        total = total + jnp.where(zi >= nl - zstep, c, self.kz)
        total = total + jnp.where(zi < zstep, c, roll(self.kz, zstep, 2))
        self.kk = total
        self.ww = DAMP / total

    def back(self, t):
        return jnp.concatenate([jnp.zeros_like(t[:1]), t[:-1]], axis=0)

    def sums(self, v):
        nxt = jnp.concatenate([v[1:], v[-1:]], axis=0)
        total = self.kx * nxt + self.back(self.kx * v)
        total = total + self.ky * roll(v, -self.ystep, 1) + roll(self.ky * v, self.ystep, 1)
        return total + self.kz * roll(v, -self.zstep, 2) + roll(self.kz * v, self.zstep, 2)

    def sweep(self, v, g):
        return KEEP * v + self.ww * (g + self.sums(v))


def halve(t, zstep):
    nx, ny, nl = t.shape
    t = t.reshape(nx // 2, 2, ny, nl)
    t = t[:, 0] + t[:, 1]
    return pairsum(pairsum(t, 1, 1), zstep, 2)


def double(t):
    nx, ny, nl = t.shape
    return jnp.broadcast_to(t[:, None], (nx, 2, ny, nl)).reshape(2 * nx, ny, nl)


def gather_line(buf, axis, me, count, sems):
    copies = []
    for d in range(1, count[axis]):
        peer = lax.rem(me[axis] + d, count[axis])
        target = (peer, me[1]) if axis == 0 else (me[0], peer)
        piece = buf.at[me[0]] if axis == 0 else buf.at[me[0], me[1]]
        copies.append(
            pltpu.make_async_remote_copy(
                src_ref=piece,
                dst_ref=piece,
                send_sem=sems.at[0, d],
                recv_sem=sems.at[1, d],
                device_id=target,
                device_id_type=MESH,
            )
        )
    for copy in copies:
        copy.start()
    return copies


def finish_line(buf, axis, me, count, sems):
    for d in range(1, count[axis]):
        peer = lax.rem(me[axis] - d + count[axis], count[axis])
        other = lax.rem(me[axis] + d, count[axis])
        target = (other, me[1]) if axis == 0 else (me[0], other)
        mine = buf.at[me[0]] if axis == 0 else buf.at[me[0], me[1]]
        piece = buf.at[peer] if axis == 0 else buf.at[me[0], peer]
        args = dict(
            send_sem=sems.at[0, d], recv_sem=sems.at[1, d], device_id=target, device_id_type=MESH
        )
        pltpu.make_async_remote_copy(src_ref=mine, dst_ref=mine, **args).wait_send()
        pltpu.make_async_remote_copy(src_ref=piece, dst_ref=piece, **args).wait_recv()


def kernel(count, levels, refs_of, table, g_in, labels, out, *scratch):
    r = refs_of(scratch)
    me = (lax.axis_index("gx"), lax.axis_index("gy"))
    axes = (me, count)
    l0, l1, l2 = levels
    bx3, by3 = l2.bx // 2, l2.by // 2

    for k, lev in enumerate(levels):
        fill(r[f"c{k}"], 1.0)
        clear_halo(lev, r[f"g{k}"])
        if k < 2:
            clear_halo(lev, r[f"p{k}"])
            fill(r[f"f{k + 1}"], 0.0)

    barrier = pltpu.get_barrier_semaphore()
    greeted = [(d, 0) for d in range(1, count[0])] + [(0, d) for d in range(1, count[1])]
    greeted += [(dx % count[0], dy % count[1]) for dx, dy in DIRS if dx and dy]
    for dx, dy in greeted:
        target = (lax.rem(me[0] + dx, count[0]), lax.rem(me[1] + dy, count[1]))
        pl.semaphore_signal(barrier, inc=1, device_id=target, device_id_type=MESH)

    fetch = pltpu.make_async_copy(
        g_in, r["g0"].at[pl.ds(l0.h, l0.bx), pl.ds(l0.h, l0.by)], r["local"]
    )
    fetch.start()

    c0, c1, c2 = r["c0"], r["c1"], r["c2"]

    def look_up(x, carry):
        lab = labels[x]
        t = jnp.zeros(lab.shape, jnp.float32)
        for klass in range(CLASSES):
            t = jnp.where(lab == klass, table[klass], t)
        c0[l0.hc + x, ROWS : ROWS + l0.by, :] = t
        return carry

    lax.fori_loop(0, l0.bx, look_up, 0)

    def put1(x, t):
        c1[l1.hc + x, ROWS : ROWS + l1.by, :] = t

    def put2(x, t):
        c2[l2.hc + x, ROWS : ROWS + l2.by, :] = t

    def put3(x, t):
        r["c3"][me[0], me[1], x * by3 : (x + 1) * by3, :] = t

    pl.semaphore_wait(barrier, len(greeted))
    e = r["ex"]
    def cond_exchange(lev, c, k):
        return exchange(
            c, c, (lev.hc, ROWS), (lev.bx, lev.by), (lev.hc, ROWS), e.at[k], axes
        )

    exc0 = cond_exchange(l0, c0, 1)
    exg0 = exchange(
        g_in, r["g0"], (l0.h,) * 2, (l0.bx, l0.by), (l0.h,) * 2, e.at[0], axes, src_offs=(0, 0)
    )
    coarsen(c0, l0.hc, l0.bx, l0.by, 1, put1)
    exc1 = cond_exchange(l1, c1, 2)
    coarsen(c1, l1.hc, l1.bx, l1.by, 2, put2)
    exc2 = cond_exchange(l2, c2, 3)
    coarsen(c2, l2.hc, l2.bx, l2.by, 4, put3)
    gather_line(r["c3"], 1, me, count, r["gat"].at[0])

    finish(exc0)
    co0 = [r[n + "0"] for n in ("kx", "ky", "kz", "kk", "ww")]
    co1 = [r[n + "1"] for n in ("kx", "ky", "kz", "kk", "ww")]
    co2 = [r[n + "2"] for n in ("kx", "ky", "kz", "kk", "ww")]
    coefficients(l0, c0, *co0, me, count)
    fetch.wait()

    relax_twice(l0, co0, r["g0"], r["a0"], r["b0"], exg0, 2)

    def down(lev, co, g, v, nxt, gn):
        def body(pair, carry):
            for key, t in restrict_rows(lev, co, g, v, pair).items():
                gn[nxt.h + pair, nxt.h + key] = t
            return carry

        lax.fori_loop(0, nxt.bx, body, 0)

    down(l0, co0, r["g0"], r["b0"], l1, r["g1"])

    def field_exchange(lev, f, k, to=None):
        to = f if to is None else to
        return exchange(f, to, (lev.h,) * 2, (lev.bx, lev.by), (lev.h,) * 2, e.at[k], axes)

    def correction_exchange(lev, f, k):
        return exchange(f, f, (1, 1), (lev.bx, lev.by), (1, 1), e.at[k], axes)

    exg1 = field_exchange(l1, r["g1"], 4)
    finish_line(r["c3"], 1, me, count, r["gat"].at[0])
    gather_line(r["c3"], 0, me, count, r["gat"].at[1])
    finish(exc1)
    finish(exc2)
    coefficients(l1, c1, *co1, me, count)
    relax_twice(l1, co1, r["g1"], r["a1"], r["b1"], exg1, 2)
    down(l1, co1, r["g1"], r["b1"], l2, r["g2"])

    exg2 = field_exchange(l2, r["g2"], 5)
    coefficients(l2, c2, *co2, me, count)
    finish(exg2)
    first_sweep(l2, co2, r["g2"], r["a2"], 3)
    sweep(l2, co2, r["g2"], r["a2"], r["b2"], 2)
    lane8 = iota((8, l2.nz), 1) % 8
    sub8 = iota((8, l2.nz), 0)
    for pair in range(bx3):
        for key, t in restrict_rows(l2, co2, r["g2"], r["b2"], pair).items():
            row = jnp.sum(jnp.where(lane8 == sub8, t, 0.0), axis=0, keepdims=True)
            at = pair * by3 + key
            r["g3"][me[0], me[1], at : at + 1, :] = row
    gather_line(r["g3"], 1, me, count, r["gat"].at[2])
    finish_line(r["c3"], 0, me, count, r["gat"].at[1])
    finish_line(r["g3"], 1, me, count, r["gat"].at[2])
    gather_line(r["g3"], 0, me, count, r["gat"].at[3])
    exp1 = field_exchange(l1, r["b1"], 6, r["p1"])
    exp0 = field_exchange(l0, r["b0"], 7, r["p0"])

    def assemble(src, dst):
        def body(x, carry):
            for y in range(count[1]):
                for k in range(bx3):
                    dst[x * bx3 + k, y * by3 : (y + 1) * by3, :] = src[
                        x, y, k * by3 : (k + 1) * by3, :
                    ]
            return carry

        lax.fori_loop(0, count[0], body, 0)

    assemble(r["c3"], r["c3w"])
    cond3 = r["c3w"][...]
    w3 = Whole(cond3, 1, 8)
    w4 = Whole(halve(cond3, 8) * 0.25, 2, 16)
    finish_line(r["g3"], 0, me, count, r["gat"].at[3])
    assemble(r["g3"], r["g3w"])
    g3 = r["g3w"][...]
    v3 = w3.ww * g3
    v3 = w3.sweep(v3, g3)
    g4 = halve(g3 + w3.sums(v3) - w3.kk * v3, 8)
    v4 = lax.fori_loop(0, SWEEPS_COARSE - 1, lambda i, v: w4.sweep(v, g4), w4.ww * g4)
    v3 = v3 + double(v4)
    v3 = w3.sweep(v3, g3)
    v3 = w3.sweep(v3, g3)
    r["v3w"][...] = v3

    xmax, ymax = count[0] * bx3 - 1, count[1] * by3 - 1
    for i in range(-1, bx3 + 1):
        x3 = jnp.clip(me[0] * bx3 + i, 0, xmax)
        for j in range(-1, by3 + 1):
            y3 = jnp.clip(me[1] * by3 + j, 0, ymax)
            row = r["v3w"][x3, pl.ds(y3, 1), :]
            t = jnp.where(lane8 == sub8, jnp.broadcast_to(row, (8, l2.nz)), 0.0)
            for step in (1, 2, 4):
                t = pairsum(t, step, 1)
            for dx in (0, 1):
                for dy in (0, 1):
                    x, y = l2.h + 2 * i + dx, l2.h + 2 * j + dy
                    r["p2"][x, y] = r["b2"][x, y] + t
    sweep(l2, co2, r["g2"], r["p2"], r["a2"], 1)
    sweep(l2, co2, r["g2"], r["a2"], r["f2"], 0, shift=l2.h - 1)

    exf2 = correction_exchange(l2, r["f2"], 9)
    add_correction(l1, r["b1"], r["f2"], r["p1"])
    sweep(l1, co1, r["g1"], r["p1"], r["a1"], 1, part=("inner", 1))
    finish(exp1)
    finish(exf2)
    add_halo(l1, r["f2"], r["p1"])
    sweep(l1, co1, r["g1"], r["p1"], r["a1"], 1, part=("rim", 1))
    sweep(l1, co1, r["g1"], r["a1"], r["f1"], 0, shift=l1.h - 1)

    exf1 = correction_exchange(l1, r["f1"], 8)
    add_correction(l0, r["b0"], r["f1"], r["p0"])
    sweep(l0, co0, r["g0"], r["p0"], r["a0"], 1, part=("inner", 1))
    finish(exp0)
    finish(exf1)
    add_halo(l0, r["f1"], r["p0"])
    sweep(l0, co0, r["g0"], r["p0"], r["a0"], 1, part=("rim", 1))
    sweep(l0, co0, r["g0"], r["a0"], out, 0, shift=l0.h)


def local(count, coil_sources, tissue_labels, class_conductivity):
    _, bx, by, nz = coil_sources.shape
    l0 = Level(0, bx, by, nz, 2, 3)
    l1 = Level(1, bx // 2, by // 2, nz, 2, 3)
    l2 = Level(2, bx // 4, by // 4, nz, 3, 4)
    f32 = jnp.float32
    shapes = {}
    for k, lev in enumerate((l0, l1, l2)):
        for name in ("g", "a", "b", "p"):
            shapes[f"{name}{k}"] = pltpu.VMEM(lev.vshape, f32)
        for name in ("c", "kx", "ky", "kz", "kk", "ww"):
            shapes[f"{name}{k}"] = pltpu.VMEM(lev.cshape, f32)
        if k:
            shapes[f"f{k}"] = pltpu.VMEM((lev.bx + 2, lev.by + 2, 8, nz), f32)
    bx3, by3 = l2.bx // 2, l2.by // 2
    whole = (count[0] * bx3, count[1] * by3, nz)
    for name in ("c3", "g3"):
        shapes[name] = pltpu.VMEM(count + (bx3 * by3, nz), f32)
        shapes[name + "w"] = pltpu.VMEM(whole, f32)
    shapes["v3w"] = pltpu.VMEM(whole, f32)
    shapes["ex"] = pltpu.SemaphoreType.DMA((10, 2, 8))
    shapes["gat"] = pltpu.SemaphoreType.DMA((4, 2, max(count)))
    shapes["local"] = pltpu.SemaphoreType.DMA
    names = list(shapes)

    columns = jnp.transpose(coil_sources, (1, 2, 0, 3))
    result = pl.pallas_call(
        functools.partial(kernel, count, (l0, l1, l2), lambda s: dict(zip(names, s))),
        out_shape=jax.ShapeDtypeStruct(columns.shape, f32),
        in_specs=[
            pl.BlockSpec(memory_space=pltpu.SMEM),
            pl.BlockSpec(memory_space=pl.ANY),
            pl.BlockSpec(memory_space=pltpu.VMEM),
        ],
        out_specs=pl.BlockSpec(memory_space=pltpu.VMEM),
        scratch_shapes=list(shapes.values()),
        compiler_params=pltpu.CompilerParams(
            collective_id=0, has_side_effects=True, vmem_limit_bytes=48 * 2**20
        ),
    )(class_conductivity, columns, tissue_labels)
    return jnp.transpose(result, (2, 0, 1, 3))


def solution(mesh):
    count = (mesh.shape["gx"], mesh.shape["gy"])
    in_specs = (P(None, "gx", "gy", None), P("gx", "gy", None), P())
    out_specs = P(None, "gx", "gy", None)
    return jax.shard_map(
        functools.partial(local, count),
        mesh=mesh,
        in_specs=in_specs,
        out_specs=out_specs,
        check_vma=False,
    )
```
